256 devices in a mesh: col: 8 (over y_hi, x), dp: 32 (over z, y_lo, core).
Axes of the slice: x: 4, y: 4 (y_hi: 2, y_lo: 2; y = y_hi * 2 + y_lo), z: 8, core: 2. Of those that a mesh axis runs over, the one named last changes fastest.
Arguments:
- stem_input: bfloat16 [4, 8192, 256], P(None, 'dp'), may hold values from -6 to 6
- top_lower: float32 [4, 8192, 256], P(None, 'dp'), may hold values from -6 to 6
- top_upper: float32 [4, 2048, 512], P(None, 'dp'), may hold values from -6 to 6
- seed_lower: bfloat16 [4, 8192, 256], P(None, 'dp'), may hold values from -6 to 6
- seed_upper: bfloat16 [4, 2048, 512], P(None, 'dp'), may hold values from -6 to 6
- gamma_lower: float32 [8, 256], P('col'), may hold values from 0.7 to 1.3
- gamma_upper: float32 [8, 512], P('col'), may hold values from 0.7 to 1.3
- lift_weight: bfloat16 [8, 512, 256], P('col'), may hold values from -0.25 to 0.25
- inner_weight: bfloat16 [8, 256, 1024], P('col'), may hold values from -0.375 to 0.375
- outer_weight: bfloat16 [8, 1024, 256], P('col'), may hold values from -0.1875 to 0.1875
- merge_weight: bfloat16 [8, 1024, 512], P('col'), may hold values from -0.1875 to 0.1875
- expand_weight: bfloat16 [8, 512, 2048], P('col'), may hold values from -0.25 to 0.25
- reduce_weight: bfloat16 [8, 2048, 512], P('col'), may hold values from -0.125 to 0.125
Outputs:
- lift_grad: float32 [8, 512, 256], P('col', 'dp')
- inner_grad: float32 [8, 256, 1024], P('col', 'dp')
- outer_grad: float32 [8, 1024, 256], P('col', 'dp')
- merge_grad: float32 [8, 1024, 512], P('col', 'dp')
- expand_grad: float32 [8, 512, 2048], P('col', 'dp')
- reduce_grad: float32 [8, 2048, 512], P('col', 'dp')
- stem_grad: float32 [4, 8192, 256], P(None, 'dp')
The draws below stay inside these ranges and needn't reach their ends.
All inputs are finite; a program needn't handle non-finite values.
Results may differ from the reference program's by a relative error of at most 0.027.
Values sent between devices are 32-bit elements; how exact they have to be, the bound alone decides.
A program may use at most 128 MiB of HBM per device.

```python
import math
import jax
import jax.numpy as jnp
from jax import lax

CL = 256
CU = 512
HL = 1024
HU = 2048
MICRO = 4
TOKU = 2048
TOKL = 8192
N_COL = 8


def level_of(own_key, shape, pieces, smallest, high):
    factor_of, own = 1.0, jax.random.fold_in(own_key, 6)
    for dim, blocks in pieces:
        steps = jnp.exp(jax.random.uniform(jax.random.fold_in(own, dim), (blocks,), jnp.float32, smallest / len(pieces), high / len(pieces)))
        factor_of = factor_of * jnp.repeat(steps, shape[dim] // blocks).reshape([-1 if axis == dim else 1 for axis in range(len(shape))])
    return factor_of


def noise(key, dims, width, limit, pieces=(), held_as=jnp.bfloat16):
    array = jax.random.normal(key, dims, jnp.float32) * width
    if len(pieces) > 0:
        array = level_of(key, dims, pieces, -0.22, 0.18) * array
    return jnp.clip(array, min=-limit, max=limit).astype(held_as)


def setup_inputs(seed: int = 0) -> dict:
    key_list = jax.random.split(jax.random.key(seed), 14)
    return {
        "stem_input": noise(key_list[0], (MICRO, TOKL, CL), 1.0, 6.0, ((1, 32),)),
        "top_lower": noise(key_list[1], (MICRO, TOKL, CL), 1.0, 6.0, ((1, 32),), jnp.float32),
        "top_upper": noise(key_list[2], (MICRO, TOKU, CU), 1.0, 6.0, ((1, 32),), jnp.float32),
        "seed_lower": noise(key_list[3], (MICRO, TOKL, CL), 1.0, 6.0, ((1, 32),)),
        "seed_upper": noise(key_list[4], (MICRO, TOKU, CU), 1.0, 6.0, ((1, 32),)),
        "gamma_lower": jnp.clip(1.0 + 0.06 * jax.random.normal(key_list[5], (N_COL, CL), jnp.float32), 0.7, 1.3),
        "gamma_upper": jnp.clip(1.0 + 0.06 * jax.random.normal(key_list[6], (N_COL, CU), jnp.float32), 0.7, 1.3),
        "lift_weight": noise(key_list[7], (N_COL, CU, CL), CU ** -0.5, 0.25, ((0, 8),)),
        "inner_weight": noise(key_list[8], (N_COL, CL, HL), CL ** -0.5, 0.375, ((0, 8),)),
        "outer_weight": noise(key_list[9], (N_COL, HL, CL), HL ** -0.5, 0.1875, ((0, 8),)),
        "merge_weight": noise(key_list[10], (N_COL, 4 * CL, CU), (4 * CL) ** -0.5, 0.1875, ((0, 8),)),
        "expand_weight": noise(key_list[11], (N_COL, CU, HU), CU ** -0.5, 0.25, ((0, 8),)),
        "reduce_weight": noise(key_list[12], (N_COL, HU, CU), HU ** -0.5, 0.125, ((0, 8),)),
    }


def normalize(values):
    return values * lax.rsqrt(lax.optimization_barrier(jnp.mean(values * values, axis=-1, keepdims=True)) + 1e-06)

def norm_back(values, cotangent):
    inverse = lax.rsqrt(lax.optimization_barrier(jnp.mean(values * values, axis=-1, keepdims=True)) + 1e-06)
    normed = values * inverse
    return inverse * (cotangent - normed * lax.optimization_barrier(jnp.mean(cotangent * normed, axis=-1, keepdims=True)))

def silu_back(hidden, cotangent):
    gate_value = jax.nn.sigmoid(hidden)
    return cotangent * gate_value * (1.0 + hidden * (1.0 - gate_value))

def product(left_side, right_side):
    return jnp.dot(left_side, right_side, preferred_element_type=jnp.float32)

def left_outer(left_side, right_side):
    return lax.dot_general(left_side, right_side, (((0,), (0,)), ((), ())), preferred_element_type=jnp.float32)

def right_outer(left_side, right_side):
    return lax.dot_general(left_side, right_side, (((1,), (1,)), ((), ())), preferred_element_type=jnp.float32)

def upper_forward(lower_cur, merge_w, expand_w, reduce_w):
    folded = lower_cur.reshape(-1, 4 * lower_cur.shape[1])
    folded_cast = normalize(folded).astype(jnp.bfloat16)
    merged = product(folded_cast, merge_w)
    merged_cast = normalize(merged).astype(jnp.bfloat16)
    hidden = product(merged_cast, expand_w)
    gated_cast = jax.nn.silu(hidden).astype(jnp.bfloat16)
    result = merged + product(gated_cast, reduce_w)
    return (result, (folded, folded_cast, merged, merged_cast, hidden, gated_cast))

def upper_backward(kept_values, cotangent, merge_w, expand_w, reduce_w):
    folded, folded_cast, merged, merged_cast, hidden, gated_cast = kept_values
    grad_cast = cotangent.astype(jnp.bfloat16)
    d_reduce = left_outer(gated_cast, grad_cast)
    hidden_cast = silu_back(hidden, right_outer(grad_cast, reduce_w)).astype(jnp.bfloat16)
    d_expand = left_outer(merged_cast, hidden_cast)
    merged_grad = (cotangent + norm_back(merged, right_outer(hidden_cast, expand_w))).astype(jnp.bfloat16)
    d_merge = left_outer(folded_cast, merged_grad)
    d_folded = norm_back(folded, right_outer(merged_grad, merge_w))
    return (d_folded.reshape(-1, d_folded.shape[1] // 4), (d_merge, d_expand, d_reduce))

def lower_forward(stem, upper_prev, lift_w, inner_w, outer_w):
    upper_cast = upper_prev.astype(jnp.bfloat16)
    lifted = product(upper_cast, lift_w)
    row_count = lifted.shape[0]
    spread = jnp.broadcast_to(lifted[:, None, :], (row_count, 4, lifted.shape[1])).reshape(row_count * 4, lifted.shape[1])
    mixed_sum = stem.astype(jnp.float32) + spread
    normed_cast = normalize(mixed_sum).astype(jnp.bfloat16)
    hidden = product(normed_cast, inner_w)
    gated_cast = jax.nn.silu(hidden).astype(jnp.bfloat16)
    result = product(gated_cast, outer_w)
    return (result, (upper_cast, mixed_sum, normed_cast, hidden, gated_cast))

def lower_backward(kept_values, cotangent, lift_w, inner_w, outer_w):
    upper_cast, mixed_sum, normed_cast, hidden, gated_cast = kept_values
    grad_cast = cotangent.astype(jnp.bfloat16)
    d_outer = left_outer(gated_cast, grad_cast)
    hidden_cast = silu_back(hidden, right_outer(grad_cast, outer_w)).astype(jnp.bfloat16)
    d_inner = left_outer(normed_cast, hidden_cast)
    d_mixed = norm_back(mixed_sum, right_outer(hidden_cast, inner_w))
    row_count = upper_cast.shape[0]
    lifted_cast = d_mixed.reshape(row_count, 4, d_mixed.shape[1]).sum(axis=1).astype(jnp.bfloat16)
    d_lift = left_outer(upper_cast, lifted_cast)
    d_upper = right_outer(lifted_cast, lift_w)
    return (d_mixed, d_upper, (d_lift, d_inner, d_outer))

def column_step(stem, lower_cur, upper_cur, grad_lower, grad_upper, gain_lower, gain_upper, weights):
    lift_w, inner_w, outer_w, merge_w, expand_w, reduce_w = weights
    upper_branch, kept_upper = upper_forward(lower_cur, merge_w, expand_w, reduce_w)
    upper_prev = (upper_cur - upper_branch) / gain_upper
    lower_branch, kept_lower = lower_forward(stem, upper_prev, lift_w, inner_w, outer_w)
    lower_prev = (lower_cur - lower_branch) / gain_lower
    from_upper, upper_grads = upper_backward(kept_upper, grad_upper, merge_w, expand_w, reduce_w)
    total_lower = grad_lower + from_upper
    d_stem, d_upper, lower_grads = lower_backward(kept_lower, total_lower, lift_w, inner_w, outer_w)
    grad_upper_prev = gain_upper * grad_upper + d_upper
    grad_lower_prev = gain_lower * total_lower
    grads = (lower_grads[0], lower_grads[1], lower_grads[2], upper_grads[0], upper_grads[1], upper_grads[2])
    return (lower_prev, upper_prev, grad_lower_prev, grad_upper_prev, grads, d_stem)

def reference(stem_input, top_lower, top_upper, seed_lower, seed_upper, gamma_lower, gamma_upper, lift_weight, inner_weight, outer_weight, merge_weight, expand_weight, reduce_weight):
    stem = stem_input.reshape(-1, CL)
    lower = top_lower.reshape(-1, CL)
    upper = top_upper.reshape(-1, CU)
    grad_lower = seed_lower.astype(jnp.float32).reshape(-1, CL)
    grad_upper = seed_upper.astype(jnp.float32).reshape(-1, CU)
    stem_sum = jnp.zeros(stem.shape, jnp.float32)
    tables = [lift_weight, inner_weight, outer_weight, merge_weight, expand_weight, reduce_weight]
    collected = [[None] * N_COL for _ in range(6)]
    for column in range(N_COL - 1, -1, -1):
        weights = tuple((table[column] for table in tables))
        lower, upper, grad_lower, grad_upper, grads, d_stem = column_step(stem, lower, upper, grad_lower, grad_upper, gamma_lower[column], gamma_upper[column], weights)
        stem_sum = stem_sum + d_stem
        for number in range(6):
            collected[number][column] = grads[number]
    factor = 1.0 / math.sqrt(MICRO * TOKL)
    outputs = [jnp.stack(collected[number]) * factor for number in range(6)]
    return (outputs[0], outputs[1], outputs[2], outputs[3], outputs[4], outputs[5], stem_sum.reshape(MICRO, TOKL, CL))
```

```python
import functools
import math

import jax
import jax.numpy as jnp
from jax import lax
from jax.experimental import pallas as pl
from jax.experimental.pallas import tpu as pltpu
from jax.sharding import PartitionSpec as P

MESH = pl.DeviceIdType.MESH
F32 = jnp.float32
BF16 = jnp.bfloat16
EPS = 1e-06
PIECES = 8
FOLD = 4
VMEM_LIMIT = 60 << 20


def product(left, right):
    return jnp.dot(left, right, preferred_element_type=F32)


def right_outer(left, right):
    return lax.dot_general(left, right, (((1,), (1,)), ((), ())), preferred_element_type=F32)


def left_outer(left, right):
    return lax.dot_general(left, right, (((0,), (0,)), ((), ())), preferred_element_type=F32)


def inverse_rms(square_sum, width):
    return lax.rsqrt(square_sum * (1.0 / width) + EPS)


def row_sum(values):
    return jnp.sum(values, axis=-1, keepdims=True)


def norm_back(values, inverse, cotangent):
    normed = values * inverse
    mean = row_sum(cotangent * normed) * (1.0 / values.shape[-1])
    return inverse * (cotangent - normed * mean)


def gate(hidden):
    return 0.5 * jnp.tanh(0.5 * hidden) + 0.5


def column_kernel(
    pieces, columns,
    stem, top_lower, top_upper, seed_lower, seed_upper, gain_lower, gain_upper,
    lift, inner, outer, merge, expand, reduce,
    folded_out, merged_out, ugate_out, gu_out, duh_out, dmerged_out,
    ucast_out, dlift_out, normed_out, lgate_out, gl_out, dlh_out, stem_out,
    in_low, in_up, in_glow, in_gup, out_low, out_up, out_glow, out_gup,
    slope_up, slope_low, stem_half, top_half, seed_half, part_half, send_sem, recv_sem, load_sem,
):
    column = lax.axis_index("col")
    first = column == columns - 1
    has_next = column > 0
    ru = in_up.shape[1]
    rl = FOLD * ru
    channels = in_low.shape[-1]
    lanes = channels // 2

    def half_copies(array, halves, index):
        return [
            pltpu.make_async_copy(
                array.at[:, pl.ds(h * lanes, lanes)], halves.at[h], load_sem.at[index, h]
            )
            for h in range(2)
        ]

    loads = half_copies(top_lower, top_half, 0)
    loads += half_copies(stem, stem_half, 1)
    loads += half_copies(seed_lower, seed_half, 2)
    for load in loads:
        load.start()

    def strided(halves, start):
        return jnp.concatenate(
            [halves[h, pl.ds(start, ru, stride=FOLD), :] for h in range(2)], axis=1
        )

    barrier = pltpu.get_barrier_semaphore()

    @pl.when(jnp.logical_not(first))
    def _():
        pl.semaphore_signal(barrier, inc=1, device_id={"col": column + 1}, device_id_type=MESH)

    @pl.when(has_next)
    def _():
        pl.semaphore_wait(barrier, 1)

    streams = ((out_low, in_low), (out_up, in_up), (out_glow, in_glow), (out_gup, in_gup))

    def copy(kind, p):
        source, target = streams[kind]
        return pltpu.make_async_remote_copy(
            src_ref=source.at[p],
            dst_ref=target.at[p],
            send_sem=send_sem.at[kind, p],
            recv_sem=recv_sem.at[kind, p],
            device_id={"col": column - 1},
            device_id_type=MESH,
        )

    def push(kind, p):
        @pl.when(has_next)
        def _():
            copy(kind, p).start()

    def arrive(kind, p):
        @pl.when(jnp.logical_not(first))
        def _():
            copy(kind, p).wait_recv()

    inverse_gain_up = 1.0 / gain_upper[...]
    inverse_gain_low = 1.0 / gain_lower[...]

    for load in loads:
        load.wait()

    def piece(p, carry):
        base = p * rl

        @pl.when(first)
        def _():
            for i in range(FOLD):
                in_low[p, i] = strided(top_half, base + i)
                in_glow[p, i] = strided(seed_half, base + i)
            in_up[p] = top_upper[p]
            in_gup[p] = seed_upper[p].astype(F32)

        arrive(0, p)
        low = [in_low[p, i] for i in range(FOLD)]
        squares = sum(row_sum(v * v) for v in low)
        inverse_fold = inverse_rms(squares, FOLD * channels)
        folded = jnp.concatenate([(v * inverse_fold).astype(BF16) for v in low], axis=1)
        folded_out[p] = folded
        merged = product(folded, merge[...])
        inverse_merged = inverse_rms(row_sum(merged * merged), merged.shape[-1])
        merged_cast = (merged * inverse_merged).astype(BF16)
        merged_out[p] = merged_cast
        branch = jnp.zeros_like(merged)
        wide = expand.shape[1]
        step = min(512, wide)
        for c in range(0, wide, step):
            hidden = product(merged_cast, expand[:, c:c + step])
            g = gate(hidden)
            gated = (hidden * g).astype(BF16)
            ugate_out[p, :, c:c + step] = gated
            slope_up[:, c:c + step] = g * (1.0 + hidden * (1.0 - g))
            branch = branch + product(gated, reduce[c:c + step, :])
        arrive(1, p)
        upper_prev = (in_up[p] - (merged + branch)) * inverse_gain_up
        out_up[p] = upper_prev
        push(1, p)
        upper_cast = upper_prev.astype(BF16)
        ucast_out[p] = upper_cast
        lifted = product(upper_cast, lift[...])
        mixed = jnp.concatenate(
            [strided(stem_half, base + i) + lifted for i in range(FOLD)], axis=0
        )
        inverse_mixed = inverse_rms(row_sum(mixed * mixed), channels)
        normed = (mixed * inverse_mixed).astype(BF16)
        normed_out[p] = normed
        wide_low = inner.shape[1]
        lower_branch = jnp.zeros((rl, channels), F32)
        step_low = min(256, wide_low)
        for c in range(0, wide_low, step_low):
            hidden = product(normed, inner[:, c:c + step_low])
            g = gate(hidden)
            gated = (hidden * g).astype(BF16)
            lgate_out[p, :, c:c + step_low] = gated
            slope_low[:, c:c + step_low] = g * (1.0 + hidden * (1.0 - g))
            lower_branch = lower_branch + product(gated, outer[c:c + step_low, :])
        for i in range(FOLD):
            out_low[p, i] = (in_low[p, i] - lower_branch[i * ru:(i + 1) * ru]) * inverse_gain_low
        push(0, p)

        arrive(3, p)
        grad_up = in_gup[p]
        gu = grad_up.astype(BF16)
        gu_out[p] = gu
        d_cast = jnp.zeros_like(merged)
        for c in range(0, wide, step):
            d_gate = right_outer(gu, reduce[c:c + step, :])
            duh = (slope_up[:, c:c + step] * d_gate).astype(BF16)
            duh_out[p, :, c:c + step] = duh
            d_cast = d_cast + right_outer(duh, expand[:, c:c + step])
        dmerged = (grad_up + norm_back(merged, inverse_merged, d_cast)).astype(BF16)
        dmerged_out[p] = dmerged
        d_fold = right_outer(dmerged, merge[...])
        low = [in_low[p, i] * inverse_fold for i in range(FOLD)]
        parts = [d_fold[:, i * channels:(i + 1) * channels] for i in range(FOLD)]
        mean = sum(row_sum(a * b) for a, b in zip(low, parts)) * (1.0 / (FOLD * channels))
        arrive(2, p)
        total = []
        for i in range(FOLD):
            t = in_glow[p, i] + inverse_fold * (parts[i] - low[i] * mean)
            out_glow[p, i] = gain_lower[...] * t
            total.append(t.astype(BF16))
        push(2, p)
        gl = jnp.concatenate(total, axis=0)
        gl_out[p] = gl
        d_normed = jnp.zeros((rl, channels), F32)
        for c in range(0, wide_low, step_low):
            d_gate = right_outer(gl, outer[c:c + step_low, :])
            dlh = (slope_low[:, c:c + step_low] * d_gate).astype(BF16)
            dlh_out[p, :, c:c + step_low] = dlh
            d_normed = d_normed + right_outer(dlh, inner[:, c:c + step_low])
        d_mixed = norm_back(mixed, inverse_mixed, d_normed)
        d_lift = jnp.zeros((ru, channels), F32)
        for i in range(FOLD):
            part = d_mixed[i * ru:(i + 1) * ru]
            for h in range(2):
                part_half[h, pl.ds(base + i, ru, stride=FOLD), :] = part[:, h * lanes:(h + 1) * lanes]
            d_lift = d_lift + part
        d_lift = d_lift.astype(BF16)
        dlift_out[p] = d_lift
        out_gup[p] = gain_upper[...] * grad_up + right_outer(d_lift, lift[...])
        push(3, p)
        return carry

    lax.fori_loop(0, pieces, piece, 0)

    stores = [
        pltpu.make_async_copy(
            part_half.at[h], stem_out.at[:, pl.ds(h * lanes, lanes)], load_sem.at[3, h]
        )
        for h in range(2)
    ]
    for store in stores:
        store.start()

    @pl.when(has_next)
    def _():
        def drain(p, carry):
            for kind in range(4):
                copy(kind, p).wait_send()
            return carry

        lax.fori_loop(0, pieces, drain, 0)

    for store in stores:
        store.wait()


def run_columns(stem, top_lower, top_upper, seed_lower, seed_upper, gain_lower, gain_upper, weights):
    pieces = PIECES
    lower_rows, channels = stem.shape
    upper_rows, width = top_upper.shape
    ru = upper_rows // pieces
    rl = lower_rows // pieces
    hidden_up = weights[4].shape[1]
    hidden_low = weights[1].shape[1]
    fold_width = FOLD * channels
    shape = lambda rows, cols, kind=BF16: jax.ShapeDtypeStruct((pieces, rows, cols), kind)
    outs = (
        shape(ru, fold_width), shape(ru, width), shape(ru, hidden_up), shape(ru, width),
        shape(ru, hidden_up), shape(ru, width), shape(ru, width), shape(ru, channels),
        shape(rl, channels), shape(rl, hidden_low), shape(rl, channels), shape(rl, hidden_low),
        jax.ShapeDtypeStruct((lower_rows, channels), F32),
    )
    low_slot = pltpu.VMEM((pieces, FOLD, ru, channels), F32)
    up_slot = pltpu.VMEM((pieces, ru, width), F32)
    vmem = pl.BlockSpec(memory_space=pltpu.VMEM)
    away = pl.BlockSpec(memory_space=pl.ANY)
    half = pltpu.VMEM((2, lower_rows, channels // 2), F32)
    results = pl.pallas_call(
        functools.partial(column_kernel, pieces, lax.axis_size("col")),
        out_shape=outs,
        in_specs=[away, away, vmem, away] + [vmem] * 9,
        out_specs=tuple([vmem] * 12 + [away]),
        scratch_shapes=[
            low_slot, up_slot, low_slot, up_slot, low_slot, up_slot, low_slot, up_slot,
            pltpu.VMEM((ru, hidden_up), F32), pltpu.VMEM((rl, hidden_low), F32),
            half, half, half, half,
            pltpu.SemaphoreType.DMA((4, pieces)), pltpu.SemaphoreType.DMA((4, pieces)),
            pltpu.SemaphoreType.DMA((4, 2)),
        ],
        compiler_params=pltpu.CompilerParams(
            collective_id=0, has_side_effects=True, vmem_limit_bytes=VMEM_LIMIT
        ),
        name="columns",
    )(
        stem.astype(F32), top_lower, top_upper.reshape(pieces, ru, width),
        seed_lower.astype(F32), seed_upper.reshape(pieces, ru, width),
        gain_lower, gain_upper, *weights,
    )
    flat = [r.reshape(-1, r.shape[-1]) for r in results]
    return flat


SLAB = 256


def scatter_kernel(
    columns, depth, factor, plan, rows_a,
    folded, merged, ugate, gu, duh, dmerged, ucast, dlift, normed, lgate, gl, dlh, stem_part,
    lift_out, inner_out, outer_out, merge_out, expand_out, reduce_out, stem_out,
    part, near, side, last, ring, stem_got,
    near_sem, side_sem, last_sem, ring_sem, stem_sem, stem_full_sem,
):
    column = lax.axis_index("col")
    place = lax.axis_index("dp")
    z, y, core = place // 4, (place // 2) % 2, place % 2
    at = lambda z, y, core: {"dp": z * 4 + y * 2 + core}
    peer = at(z, y, 1 - core)
    across = at(z, 1 - y, core)
    toward = (at((z + 1) % depth, y, core), at((z + depth - 1) % depth, y, core))
    others = [(column + d) % columns for d in range(1, columns)]

    barrier = pltpu.get_barrier_semaphore()
    for target in (peer, across) + toward + tuple({"col": o} for o in others):
        pl.semaphore_signal(barrier, inc=1, device_id=target, device_id_type=MESH)
    pl.semaphore_wait(barrier, 3 + columns)

    def remote(source, target, send, recv, device):
        return pltpu.make_async_remote_copy(
            src_ref=source, dst_ref=target, send_sem=send, recv_sem=recv,
            device_id=device, device_id_type=MESH,
        )

    def weight_grad(name):
        left, right, start = {
            "reduce": (ugate, gu, plan["reduce"]), "expand": (merged, duh, plan["expand"]),
            "merge": (folded, dmerged, plan["merge"]), "outer": (lgate, gl, plan["outer"]),
            "inner": (normed, dlh, plan["inner"]), "lift": (ucast, dlift, plan["lift"]),
        }[name]
        height, width = left.shape[1], right.shape[1]
        block = height // (4 * depth)
        for top in range(0, height, SLAB):
            grad = left_outer(left[:, top:top + SLAB], right[...])
            count = SLAB // (4 * block)
            z0 = top // (4 * block)
            for slab in range(width // SLAB):
                piece = grad[:, slab * SLAB:(slab + 1) * SLAB].reshape(count, 2, 2, block, SLAB)
                rows = slice(start + slab * block, start + (slab + 1) * block)
                for yb in range(2):
                    part[yb * depth + z0:yb * depth + z0 + count, :, rows, :] = piece[:, yb]

    def near_copy(group):
        start, rows, _ = group
        return remote(
            part.at[:, 1 - core, pl.ds(start, rows)], near.at[:, pl.ds(start, rows)],
            near_sem.at[0, start // 16], near_sem.at[1, start // 16], peer,
        )

    def side_copy(group):
        start, rows, _ = group
        return remote(
            near.at[pl.ds((1 - y) * depth, depth), pl.ds(start, rows)],
            side.at[:, pl.ds(start - rows_a, rows)],
            side_sem.at[0, start // 16], side_sem.at[1, start // 16], across,
        )

    def flows(group):
        start, rows, first = group
        if first:
            return [(way, start, rows, way, start) for way in range(2)]
        half = rows // 2
        slot = rows_a + (start - rows_a) // 2
        return [(way, start + way * half, half, y, slot) for way in range(2)]

    def block_at(way, step):
        if way == 0:
            return (z + 2 * depth - 1 - step) % depth
        return (z + 1 + step) % depth

    def gathered(group, flow, step, zb):
        way, start, rows, yb, slot = flow
        value = near[yb * depth + zb, start:start + rows] + part[yb * depth + zb, core, start:start + rows]
        if not group[2]:
            value = value + side[zb, start - rows_a:start - rows_a + rows]
        return value

    def ring_copy(flow, step):
        way, start, rows, yb, slot = flow
        return remote(
            near.at[yb * depth + block_at(way, step), pl.ds(start, rows)],
            ring.at[way, step, pl.ds(slot, rows)],
            ring_sem.at[0, way, step, slot // 16], ring_sem.at[1, way, step, slot // 16], toward[way],
        )

    def ring_step(group, step, opening):
        for flow in flows(group):
            way, start, rows, yb, slot = flow
            zb = block_at(way, step)
            value = gathered(group, flow, step, zb)
            if not opening:
                ring_copy(flow, step - 1).wait_recv()
                value = value + ring[way, step - 1, slot:slot + rows]
            near[yb * depth + zb, start:start + rows] = value
            ring_copy(flow, step).start()

    def ring_end(group):
        for flow in flows(group):
            way, start, rows, yb, slot = flow
            ring_copy(flow, depth - 2).wait_recv()
            value = gathered(group, flow, depth - 1, z)
            near[yb * depth + z, start:start + rows] = value + ring[way, depth - 2, slot:slot + rows]

    def side_open(group):
        start, rows, _ = group

        def add(zb, carry):
            b = (1 - y) * depth + zb
            near[b, start:start + rows] = near[b, start:start + rows] + part[b, core, start:start + rows]
            return carry

        lax.fori_loop(0, depth, add, 0)
        side_copy(group).start()

    a1, a2 = (0, plan["outer"], True), (plan["outer"], rows_a - plan["outer"], True)
    b1 = (rows_a, plan["merge"] - rows_a, False)
    b2 = (plan["merge"], part.shape[2] - plan["merge"], False)

    weight_grad("reduce")
    near_copy(a1).start()
    weight_grad("expand")
    near_copy(b1).start()
    near_copy(a1).wait_recv()
    ring_step(a1, 0, True)
    weight_grad("merge")
    near_copy(b2).start()
    near_copy(b1).wait_recv()
    side_open(b1)
    for name in ("outer", "inner", "lift"):
        weight_grad(name)
    near_copy(a2).start()
    near_copy(b2).wait_recv()
    side_open(b2)
    near_copy(a2).wait_recv()
    ring_step(a2, 0, True)

    seg = stem_part.shape[0] // columns

    def stem_copy(owner, slot_of):
        return remote(
            stem_part.at[pl.ds(owner * seg, seg)], stem_got.at[0, slot_of],
            stem_sem.at[0, owner], stem_sem.at[1, slot_of], {"col": owner},
        )

    def stem_spread(target, slot_of):
        return remote(
            stem_got.at[1, column], stem_got.at[1, slot_of],
            stem_full_sem.at[0, target], stem_full_sem.at[1, slot_of], {"col": target},
        )

    for other in others:
        stem_copy(other, column).start()

    def first_rings(step, carry):
        ring_step(a1, step, False)
        ring_step(a2, step, False)
        return carry

    lax.fori_loop(1, depth - 1, first_rings, 0)

    for group in (b1, b2):
        side_copy(group).wait_recv()
        ring_step(group, 0, True)
    ring_end(a1)
    ring_end(a2)
    last_copy = remote(
        near.at[(1 - y) * depth + z, pl.ds(0, rows_a)], last, last_sem.at[0], last_sem.at[1], across
    )
    last_copy.start()

    total = stem_part[pl.ds(pl.multiple_of(column * seg, seg), seg), :]
    for other in others:
        stem_copy(other, other).wait_recv()
        total = total + stem_got[0, other]
    stem_got[1, column] = total
    for other in others:
        stem_spread(other, column).start()

    def second_rings(step, carry):
        ring_step(b1, step, False)
        ring_step(b2, step, False)
        return carry

    lax.fori_loop(1, depth - 1, second_rings, 0)

    def emit(out, name, value):
        block, width = out.shape
        start = plan[name] - value[1]
        for slab in range(width // SLAB):
            out[:, slab * SLAB:(slab + 1) * SLAB] = (
                value[0][start + slab * block:start + (slab + 1) * block] * factor
            )

    last_copy.wait_recv()
    mine = near[y * depth + z, 0:rows_a] + last[...]
    for out, name in ((reduce_out, "reduce"), (outer_out, "outer"), (inner_out, "inner"), (lift_out, "lift")):
        emit(out, name, (mine, 0))
    ring_end(b1)
    ring_end(b2)
    mine = near[y * depth + z, rows_a:part.shape[2]]
    for out, name in ((expand_out, "expand"), (merge_out, "merge")):
        emit(out, name, (mine, rows_a))

    stem_out[pl.ds(pl.multiple_of(column * seg, seg), seg), :] = stem_got[1, column]
    for other in others:
        stem_spread(other, other).wait_recv()
        stem_out[pl.ds(pl.multiple_of(other * seg, seg), seg), :] = stem_got[1, other]

    for group in (a1, a2, b1, b2):
        near_copy(group).wait_send()
    for group in (b1, b2):
        side_copy(group).wait_send()
    last_copy.wait_send()

    def drain(step, carry):
        for group in (a1, a2, b1, b2):
            for flow in flows(group):
                ring_copy(flow, step).wait_send()
        return carry

    lax.fori_loop(0, depth - 1, drain, 0)
    for other in others:
        stem_copy(other, column).wait_send()
        stem_spread(other, column).wait_send()


def run_scatter(saved, shapes, factor):
    devices = lax.axis_size("dp")
    columns = lax.axis_size("col")
    depth = devices // 4
    blocks = [(rows // devices, cols) for rows, cols in shapes]
    heights = {
        name: block * (cols // SLAB)
        for name, (block, cols) in zip(("lift", "inner", "outer", "merge", "expand", "reduce"), blocks)
    }
    plan, height = {}, 0
    for name in ("reduce", "outer", "inner", "lift", "expand", "merge"):
        plan[name] = height
        height += heights[name]
    rows_a = plan["expand"]
    slots = rows_a + (height - rows_a) // 2
    stem_part = saved[-1]
    outs = [jax.ShapeDtypeStruct(b, F32) for b in blocks]
    outs.append(jax.ShapeDtypeStruct(stem_part.shape, F32))
    seg = stem_part.shape[0] // columns
    vmem = pl.BlockSpec(memory_space=pltpu.VMEM)
    dma = pltpu.SemaphoreType.DMA
    return pl.pallas_call(
        functools.partial(scatter_kernel, columns, depth, factor, plan, rows_a),
        out_shape=tuple(outs),
        in_specs=[vmem] * 13,
        out_specs=tuple(vmem for _ in outs),
        scratch_shapes=[
            pltpu.VMEM((2 * depth, 2, height, SLAB), F32),
            pltpu.VMEM((2 * depth, height, SLAB), F32),
            pltpu.VMEM((depth, height - rows_a, SLAB), F32),
            pltpu.VMEM((rows_a, SLAB), F32),
            pltpu.VMEM((2, depth - 1, slots, SLAB), F32),
            pltpu.VMEM((2, columns, seg, stem_part.shape[1]), F32),
            dma((2, 32)), dma((2, 32)), dma((2,)), dma((2, 2, depth, 32)),
            dma((2, columns)), dma((2, columns)),
        ],
        compiler_params=pltpu.CompilerParams(
            collective_id=1, has_side_effects=True, vmem_limit_bytes=VMEM_LIMIT
        ),
        name="scatter",
    )(*saved)


def shards(stem_input, top_lower, top_upper, seed_lower, seed_upper, gamma_lower, gamma_upper, *weights):
    flat = lambda array: array.reshape(-1, array.shape[-1])
    weights = [w[0] for w in weights]
    saved = run_columns(
        flat(stem_input), flat(top_lower), flat(top_upper), flat(seed_lower), flat(seed_upper),
        gamma_lower, gamma_upper, weights,
    )
    factor = 1.0 / math.sqrt(saved[-1].shape[0] * lax.axis_size("dp"))
    results = run_scatter(saved, [w.shape for w in weights], factor)
    return tuple(r[None] for r in results[:6]) + (results[6].reshape(stem_input.shape),)


def solution(mesh):
    spread = P(None, "dp", None)
    gains = P("col", None)
    table = P("col", None, None)
    in_specs = (spread,) * 5 + (gains,) * 2 + (table,) * 6
    out_specs = (P("col", "dp", None),) * 6 + (spread,)
    return jax.shard_map(shards, mesh=mesh, in_specs=in_specs, out_specs=out_specs, check_vma=False)
```

```python
import functools
import math

import jax
import jax.numpy as jnp
from jax import lax
from jax.experimental import pallas as pl
from jax.experimental.pallas import tpu as pltpu
from jax.sharding import PartitionSpec as P

MESH = pl.DeviceIdType.MESH
F32 = jnp.float32
BF16 = jnp.bfloat16
EPS = 1e-06
PIECES = 16
FOLD = 4
VMEM_LIMIT = 60 << 20


def product(left, right):
    return jnp.dot(left, right, preferred_element_type=F32)


def right_outer(left, right):
    return lax.dot_general(left, right, (((1,), (1,)), ((), ())), preferred_element_type=F32)


def left_outer(left, right):
    return lax.dot_general(left, right, (((0,), (0,)), ((), ())), preferred_element_type=F32)


def inverse_rms(square_sum, width):
    return lax.rsqrt(square_sum * (1.0 / width) + EPS)


def row_sum(values):
    return jnp.sum(values, axis=-1, keepdims=True)


def norm_back(values, inverse, cotangent):
    normed = values * inverse
    mean = row_sum(cotangent * normed) * (1.0 / values.shape[-1])
    return inverse * (cotangent - normed * mean)


def gate(hidden):
    return 0.5 * jnp.tanh(0.5 * hidden) + 0.5


def column_kernel(
    pieces, columns,
    stem, top_lower, top_upper, seed_lower, seed_upper, gain_lower, gain_upper,
    lift, inner, outer, merge, expand, reduce,
    folded_out, merged_out, ugate_out, gu_out, duh_out, dmerged_out,
    ucast_out, dlift_out, normed_out, lgate_out, gl_out, dlh_out, stem_out,
    in_low, in_up, in_glow, in_gup, out_low, out_up, out_glow, out_gup,
    slope_up, slope_low, top_half, part_half, send_sem, recv_sem, load_sem,
):
    column = lax.axis_index("col")
    first = column == columns - 1
    has_next = column > 0
    ru = in_up.shape[1]
    rl = FOLD * ru
    channels = in_low.shape[-1]
    lanes = channels // 2

    def half_copies(array, halves, index):
        return [
            pltpu.make_async_copy(
                array.at[:, pl.ds(h * lanes, lanes)], halves.at[h], load_sem.at[index, h]
            )
            for h in range(2)
        ]

    loads = half_copies(top_lower, top_half, 0)

    @pl.when(first)
    def _():
        for load in loads:
            load.start()

    def strided(halves, start):
        return jnp.concatenate(
            [halves[h, pl.ds(start, ru, stride=FOLD), :] for h in range(2)], axis=1
        )

    barrier = pltpu.get_barrier_semaphore()

    @pl.when(jnp.logical_not(first))
    def _():
        pl.semaphore_signal(barrier, inc=1, device_id={"col": column + 1}, device_id_type=MESH)

    @pl.when(has_next)
    def _():
        pl.semaphore_wait(barrier, 1)

    streams = ((out_low, in_low), (out_up, in_up), (out_glow, in_glow), (out_gup, in_gup))

    def copy(kind, p):
        source, target = streams[kind]
        return pltpu.make_async_remote_copy(
            src_ref=source.at[p],
            dst_ref=target.at[p],
            send_sem=send_sem.at[kind, p],
            recv_sem=recv_sem.at[kind, p],
            device_id={"col": column - 1},
            device_id_type=MESH,
        )

    def push(kinds, p):
        @pl.when(has_next)
        def _():
            for kind in kinds:
                copy(kind, p).start()

    def arrive(kind, p):
        @pl.when(jnp.logical_not(first))
        def _():
            copy(kind, p).wait_recv()

    inverse_gain_up = 1.0 / gain_upper[...]
    inverse_gain_low = 1.0 / gain_lower[...]

    @pl.when(first)
    def _():
        for load in loads:
            load.wait()

    spot = lax.broadcasted_iota(jnp.int32, (rl, rl), 0)
    token = lax.broadcasted_iota(jnp.int32, (rl, rl), 1)
    order = jnp.where(token == (spot % ru) * FOLD + spot // ru, 1.0, 0.0).astype(BF16)

    def piece(p, carry):
        base = p * rl

        @pl.when(first)
        def _():
            seeds = product(order, seed_lower[p])
            for i in range(FOLD):
                in_low[p, i] = strided(top_half, base + i)
                in_glow[p, i] = seeds[i * ru:(i + 1) * ru]
            in_up[p] = top_upper[p]
            in_gup[p] = seed_upper[p].astype(F32)

        arrive(0, p)
        low = [in_low[p, i] for i in range(FOLD)]
        squares = sum(row_sum(v * v) for v in low)
        inverse_fold = inverse_rms(squares, FOLD * channels)
        folded = jnp.concatenate([(v * inverse_fold).astype(BF16) for v in low], axis=1)
        folded_out[p] = folded
        merged = product(folded, merge[...])
        inverse_merged = inverse_rms(row_sum(merged * merged), merged.shape[-1])
        merged_cast = (merged * inverse_merged).astype(BF16)
        merged_out[p] = merged_cast
        branch = jnp.zeros_like(merged)
        wide = expand.shape[1]
        step = wide
        for c in range(0, wide, step):
            hidden = product(merged_cast, expand[:, c:c + step])
            g = gate(hidden)
            gated = (hidden * g).astype(BF16)
            ugate_out[p, :, c:c + step] = gated
            slope_up[:, c:c + step] = g * (1.0 + hidden * (1.0 - g))
            branch = branch + product(gated, reduce[c:c + step, :])
        arrive(1, p)
        upper_prev = (in_up[p] - (merged + branch)) * inverse_gain_up
        out_up[p] = upper_prev
        upper_cast = upper_prev.astype(BF16)
        ucast_out[p] = upper_cast
        lifted = product(upper_cast, lift[...])
        mixed = product(order, stem[p]) + jnp.concatenate([lifted] * FOLD, axis=0)
        inverse_mixed = inverse_rms(row_sum(mixed * mixed), channels)
        normed = (mixed * inverse_mixed).astype(BF16)
        normed_out[p] = normed
        wide_low = inner.shape[1]
        lower_branch = jnp.zeros((rl, channels), F32)
        step_low = wide_low
        for c in range(0, wide_low, step_low):
            hidden = product(normed, inner[:, c:c + step_low])
            g = gate(hidden)
            gated = (hidden * g).astype(BF16)
            lgate_out[p, :, c:c + step_low] = gated
            slope_low[:, c:c + step_low] = g * (1.0 + hidden * (1.0 - g))
            lower_branch = lower_branch + product(gated, outer[c:c + step_low, :])
        for i in range(FOLD):
            out_low[p, i] = (in_low[p, i] - lower_branch[i * ru:(i + 1) * ru]) * inverse_gain_low
        push((0, 1), p)

        arrive(3, p)
        grad_up = in_gup[p]
        gu = grad_up.astype(BF16)
        gu_out[p] = gu
        d_cast = jnp.zeros_like(merged)
        for c in range(0, wide, step):
            d_gate = right_outer(gu, reduce[c:c + step, :])
            duh = (slope_up[:, c:c + step] * d_gate).astype(BF16)
            duh_out[p, :, c:c + step] = duh
            d_cast = d_cast + right_outer(duh, expand[:, c:c + step])
        dmerged = (grad_up + norm_back(merged, inverse_merged, d_cast)).astype(BF16)
        dmerged_out[p] = dmerged
        d_fold = right_outer(dmerged, merge[...])
        low = [in_low[p, i] * inverse_fold for i in range(FOLD)]
        parts = [d_fold[:, i * channels:(i + 1) * channels] for i in range(FOLD)]
        mean = sum(row_sum(a * b) for a, b in zip(low, parts)) * (1.0 / (FOLD * channels))
        arrive(2, p)
        total = []
        for i in range(FOLD):
            t = in_glow[p, i] + inverse_fold * (parts[i] - low[i] * mean)
            out_glow[p, i] = gain_lower[...] * t
            total.append(t.astype(BF16))
        gl = jnp.concatenate(total, axis=0)
        gl_out[p] = gl
        d_normed = jnp.zeros((rl, channels), F32)
        for c in range(0, wide_low, step_low):
            d_gate = right_outer(gl, outer[c:c + step_low, :])
            dlh = (slope_low[:, c:c + step_low] * d_gate).astype(BF16)
            dlh_out[p, :, c:c + step_low] = dlh
            d_normed = d_normed + right_outer(dlh, inner[:, c:c + step_low])
        d_mixed = norm_back(mixed, inverse_mixed, d_normed)
        d_lift = jnp.zeros((ru, channels), F32)
        for i in range(FOLD):
            part = d_mixed[i * ru:(i + 1) * ru]
            for h in range(2):
                part_half[h, pl.ds(base + i, ru, stride=FOLD), :] = part[:, h * lanes:(h + 1) * lanes]
            d_lift = d_lift + part
        d_lift = d_lift.astype(BF16)
        dlift_out[p] = d_lift
        out_gup[p] = gain_upper[...] * grad_up + right_outer(d_lift, lift[...])
        push((3, 2), p)
        return carry

    lax.fori_loop(0, pieces, piece, 0)

    stores = [
        pltpu.make_async_copy(
            part_half.at[h], stem_out.at[:, pl.ds(h * lanes, lanes)], load_sem.at[1, h]
        )
        for h in range(2)
    ]
    for store in stores:
        store.start()

    @pl.when(has_next)
    def _():
        def drain(p, carry):
            for kind in range(4):
                copy(kind, p).wait_send()
            return carry

        lax.fori_loop(0, pieces, drain, 0)

    for store in stores:
        store.wait()


def run_columns(stem, top_lower, top_upper, seed_lower, seed_upper, gain_lower, gain_upper, weights):
    pieces = PIECES
    lower_rows, channels = stem.shape
    upper_rows, width = top_upper.shape
    ru = upper_rows // pieces
    rl = lower_rows // pieces
    hidden_up = weights[4].shape[1]
    hidden_low = weights[1].shape[1]
    fold_width = FOLD * channels
    shape = lambda rows, cols, kind=BF16: jax.ShapeDtypeStruct((pieces, rows, cols), kind)
    outs = (
        shape(ru, fold_width), shape(ru, width), shape(ru, hidden_up), shape(ru, width),
        shape(ru, hidden_up), shape(ru, width), shape(ru, width), shape(ru, channels),
        shape(rl, channels), shape(rl, hidden_low), shape(rl, channels), shape(rl, hidden_low),
        jax.ShapeDtypeStruct((lower_rows, channels), F32),
    )
    low_slot = pltpu.VMEM((pieces, FOLD, ru, channels), F32)
    up_slot = pltpu.VMEM((pieces, ru, width), F32)
    vmem = pl.BlockSpec(memory_space=pltpu.VMEM)
    away = pl.BlockSpec(memory_space=pl.ANY)
    half = pltpu.VMEM((2, lower_rows, channels // 2), F32)
    results = pl.pallas_call(
        functools.partial(column_kernel, pieces, lax.axis_size("col")),
        out_shape=outs,
        in_specs=[vmem, away] + [vmem] * 11,
        out_specs=tuple([vmem] * 12 + [away]),
        scratch_shapes=[
            low_slot, up_slot, low_slot, up_slot, low_slot, up_slot, low_slot, up_slot,
            pltpu.VMEM((ru, hidden_up), F32), pltpu.VMEM((rl, hidden_low), F32),
            half, half,
            pltpu.SemaphoreType.DMA((4, pieces)), pltpu.SemaphoreType.DMA((4, pieces)),
            pltpu.SemaphoreType.DMA((2, 2)),
        ],
        compiler_params=pltpu.CompilerParams(
            collective_id=0, has_side_effects=True, vmem_limit_bytes=VMEM_LIMIT
        ),
        name="columns",
    )(
        stem.reshape(pieces, rl, channels), top_lower, top_upper.reshape(pieces, ru, width),
        seed_lower.reshape(pieces, rl, channels), seed_upper.reshape(pieces, ru, width),
        gain_lower, gain_upper, *weights,
    )
    flat = [r.reshape(-1, r.shape[-1]) for r in results]
    return flat


SLAB = 256


def scatter_kernel(
    columns, depth, factor, plan, rows_a,
    folded, merged, ugate, gu, duh, dmerged, ucast, dlift, normed, lgate, gl, dlh, stem_part,
    packed_out, stem_out,
    part, near, side, last, ring, stem_got, stem_half, stem_full,
    near_sem, side_sem, last_sem, ring_sem, row_sem, half_sem, full_sem, out_sem,
):
    column = lax.axis_index("col")
    place = lax.axis_index("dp")
    z, y, core = place // 4, (place // 2) % 2, place % 2
    at = lambda z, y, core: {"dp": z * 4 + y * 2 + core}
    peer = at(z, y, 1 - core)
    across = at(z, 1 - y, core)
    toward = (at((z + 1) % depth, y, core), at((z + depth - 1) % depth, y, core))
    row = columns // 2
    x, high = column % row, column // row
    mates = [(x + d) % row for d in range(1, row)]
    mate = lambda other: {"col": high * row + other}
    mirror = {"col": (1 - high) * row + x}

    barrier = pltpu.get_barrier_semaphore()
    for target in (peer, across, mirror) + toward + tuple(mate(o) for o in mates):
        pl.semaphore_signal(barrier, inc=1, device_id=target, device_id_type=MESH)
    pl.semaphore_wait(barrier, 4 + row)

    def remote(source, target, send, recv, device):
        return pltpu.make_async_remote_copy(
            src_ref=source, dst_ref=target, send_sem=send, recv_sem=recv,
            device_id=device, device_id_type=MESH,
        )

    def weight_grad(name):
        left, right, start = {
            "reduce": (ugate, gu, plan["reduce"]), "expand": (merged, duh, plan["expand"]),
            "merge": (folded, dmerged, plan["merge"]), "outer": (lgate, gl, plan["outer"]),
            "inner": (normed, dlh, plan["inner"]), "lift": (ucast, dlift, plan["lift"]),
        }[name]
        height, width = left.shape[1], right.shape[1]
        block = height // (4 * depth)
        for top in range(0, height, SLAB):
            grad = left_outer(left[:, top:top + SLAB], right[...])
            count = SLAB // (4 * block)
            z0 = top // (4 * block)
            for slab in range(width // SLAB):
                piece = grad[:, slab * SLAB:(slab + 1) * SLAB].reshape(count, 2, 2, block, SLAB)
                rows = slice(start + slab * block, start + (slab + 1) * block)
                for yb in range(2):
                    part[yb * depth + z0:yb * depth + z0 + count, :, rows, :] = piece[:, yb]

    a1, a2 = (0, plan["outer"], True), (plan["outer"], rows_a - plan["outer"], True)
    b1 = (rows_a, plan["merge"] - rows_a, False)
    b2 = (plan["merge"], part.shape[2] - plan["merge"], False)

    def near_copy(group):
        start, rows, _ = group
        return remote(
            part.at[:, 1 - core, pl.ds(start, rows)], near.at[:, pl.ds(start, rows)],
            near_sem.at[0, start // 16], near_sem.at[1, start // 16], peer,
        )

    def side_copy(group):
        start, rows, _ = group
        return remote(
            near.at[pl.ds((1 - y) * depth, depth), pl.ds(start, rows)],
            side.at[:, pl.ds(start - rows_a, rows)],
            side_sem.at[0, start // 16], side_sem.at[1, start // 16], across,
        )

    def flows(group):
        start, rows, first = group
        found = []
        for lane in range(2):
            for way in range(2):
                steps = depth // 2 if way == lane else depth // 2 - 1
                if first:
                    found.append((way, lane, steps, start, rows, lane, start))
                else:
                    half = rows // 2
                    slot = rows_a + (start - rows_a) // 2
                    found.append((way, lane, steps, start + lane * half, half, y, slot))
        return found

    def block_at(flow, step):
        way, steps = flow[0], flow[2]
        if way == 0:
            return (z + steps - step) % depth
        return (z + depth - steps + step) % depth

    def gathered(group, flow, zb):
        way, lane, steps, start, rows, yb, slot = flow
        value = near[yb * depth + zb, start:start + rows] + part[yb * depth + zb, core, start:start + rows]
        if not group[2]:
            value = value + side[zb, start - rows_a:start - rows_a + rows]
        return value

    def ring_copy(flow, step):
        way, lane, steps, start, rows, yb, slot = flow
        return remote(
            near.at[yb * depth + block_at(flow, step), pl.ds(start, rows)],
            ring.at[way, lane, step, pl.ds(slot, rows)],
            ring_sem.at[0, way, lane, step, slot // 16], ring_sem.at[1, way, lane, step, slot // 16],
            toward[way],
        )

    def ring_step(group, step):
        for flow in flows(group):
            way, lane, steps, start, rows, yb, slot = flow
            if step >= steps:
                continue
            zb = block_at(flow, step)
            value = gathered(group, flow, zb)
            if step > 0:
                ring_copy(flow, step - 1).wait_recv()
                value = value + ring[way, lane, step - 1, slot:slot + rows]
            near[yb * depth + zb, start:start + rows] = value
            ring_copy(flow, step).start()

    def ring_end(group):
        found = flows(group)
        for lane in range(2):
            pair = [flow for flow in found if flow[1] == lane]
            way, lane, steps, start, rows, yb, slot = pair[0]
            value = gathered(group, pair[0], z)
            for flow in pair:
                ring_copy(flow, flow[2] - 1).wait_recv()
                value = value + ring[flow[0], lane, flow[2] - 1, slot:slot + rows]
            near[yb * depth + z, start:start + rows] = value

    def side_open(group):
        start, rows, _ = group

        def add(zb, carry):
            b = (1 - y) * depth + zb
            near[b, start:start + rows] = near[b, start:start + rows] + part[b, core, start:start + rows]
            return carry

        lax.fori_loop(0, depth, add, 0)
        side_copy(group).start()

    a1, a2 = (0, plan["outer"], True), (plan["outer"], rows_a - plan["outer"], True)
    b1 = (rows_a, plan["merge"] - rows_a, False)
    b2 = (plan["merge"], part.shape[2] - plan["merge"], False)

    quarter = stem_part.shape[0] // row
    half = quarter // 2
    span = lambda index, size: pl.ds(pl.multiple_of(index * size, size), size)

    def row_copy(target, slot):
        return remote(
            stem_part.at[span(target, quarter)], stem_got.at[slot],
            row_sem.at[0, target], row_sem.at[1, slot], mate(target),
        )

    half_copy = remote(
        stem_half.at[0, span(1 - high, half)], stem_half.at[1, pl.ds(0, half)],
        half_sem.at[0], half_sem.at[1], mirror,
    )

    def back_copy(part_of):
        ref = stem_full.at[x, span(part_of, half)]
        return remote(ref, ref, half_sem.at[2], half_sem.at[3], mirror)

    def full_copy(target, slot):
        ref = stem_full.at[slot]
        return remote(ref, ref, full_sem.at[0, target], full_sem.at[1, slot], mate(target))

    def stem_rows():
        total = stem_part[span(x, quarter), :]
        for other in mates:
            row_copy(other, other).wait_recv()
            total = total + stem_got[other]
        stem_half[0] = total
        half_copy.start()

    def stem_mirror():
        half_copy.wait_recv()
        stem_full[x, span(high, half), :] = stem_half[0, span(high, half), :] + stem_half[1, 0:half]
        back_copy(high).start()

    def stem_spread():
        back_copy(1 - high).wait_recv()
        for other in mates:
            full_copy(other, x).start()

    for other in mates:
        row_copy(other, x).start()
    weight_grad("expand")
    near_copy(b1).start()
    weight_grad("reduce")
    near_copy(a1).start()
    near_copy(b1).wait_recv()
    side_open(b1)
    weight_grad("merge")
    near_copy(b2).start()
    near_copy(a1).wait_recv()
    ring_step(a1, 0)
    for name in ("outer", "inner", "lift"):
        weight_grad(name)
    near_copy(a2).start()
    near_copy(b2).wait_recv()
    side_open(b2)
    near_copy(a2).wait_recv()
    ring_step(a2, 0)
    ring_step(a1, 1)
    ring_step(a2, 1)
    ring_step(a1, 2)
    ring_step(a2, 2)
    stem_rows()
    side_copy(b1).wait_recv()
    ring_step(b1, 0)
    ring_step(a1, 3)
    ring_step(a2, 3)
    stem_mirror()
    ring_step(b1, 1)
    ring_end(a1)
    ring_end(a2)
    last_copy = remote(
        near.at[(1 - y) * depth + z, pl.ds(0, rows_a)], last, last_sem.at[0], last_sem.at[1], across
    )
    last_copy.start()
    stem_spread()
    side_copy(b2).wait_recv()
    ring_step(b2, 0)
    for step in range(2, depth // 2):
        ring_step(b1, step)
        ring_step(b2, step - 1)
    ring_step(b2, depth // 2 - 1)
    for other in mates:
        full_copy(other, other).wait_recv()
    stem_store = pltpu.make_async_copy(stem_full, stem_out, out_sem)
    stem_store.start()
    last_copy.wait_recv()
    packed_out[0:rows_a] = (near[y * depth + z, 0:rows_a] + last[...]) * factor
    ring_end(b1)
    ring_end(b2)
    packed_out[rows_a:] = near[y * depth + z, rows_a:] * factor

    for group in (a1, a2, b1, b2):
        near_copy(group).wait_send()
        for flow in flows(group):
            for step in range(flow[2]):
                ring_copy(flow, step).wait_send()
    for group in (b1, b2):
        side_copy(group).wait_send()
    last_copy.wait_send()
    half_copy.wait_send()
    back_copy(high).wait_send()
    for other in mates:
        row_copy(other, x).wait_send()
        full_copy(other, x).wait_send()
    stem_store.wait()


def run_scatter(saved, shapes, factor):
    devices = lax.axis_size("dp")
    columns = lax.axis_size("col")
    depth = devices // 4
    blocks = [(rows // devices, cols) for rows, cols in shapes]
    heights = {
        name: block * (cols // SLAB)
        for name, (block, cols) in zip(("lift", "inner", "outer", "merge", "expand", "reduce"), blocks)
    }
    plan, height = {}, 0
    for name in ("reduce", "outer", "inner", "lift", "expand", "merge"):
        plan[name] = height
        height += heights[name]
    rows_a = plan["expand"]
    slots = rows_a + (height - rows_a) // 2
    row = columns // 2
    stem_part = saved[-1]
    quarter = (stem_part.shape[0] // row, stem_part.shape[1])
    full = (row,) + quarter
    vmem = pl.BlockSpec(memory_space=pltpu.VMEM)
    away = pl.BlockSpec(memory_space=pl.ANY)
    dma = pltpu.SemaphoreType.DMA
    packed, stem = pl.pallas_call(
        functools.partial(scatter_kernel, columns, depth, factor, plan, rows_a),
        out_shape=(jax.ShapeDtypeStruct((height, SLAB), F32), jax.ShapeDtypeStruct(full, F32)),
        in_specs=[vmem] * 13,
        out_specs=(vmem, away),
        scratch_shapes=[
            pltpu.VMEM((2 * depth, 2, height, SLAB), F32),
            pltpu.VMEM((2 * depth, height, SLAB), F32),
            pltpu.VMEM((depth, height - rows_a, SLAB), F32),
            pltpu.VMEM((rows_a, SLAB), F32),
            pltpu.VMEM((2, 2, depth // 2, slots, SLAB), F32),
            pltpu.VMEM(full, F32), pltpu.VMEM((2,) + quarter, F32), pltpu.VMEM(full, F32),
            dma((2, 32)), dma((2, 32)), dma((2,)), dma((2, 2, 2, depth // 2, 32)),
            dma((2, row)), dma((4,)), dma((2, row)), dma,
        ],
        compiler_params=pltpu.CompilerParams(
            collective_id=1, has_side_effects=True, vmem_limit_bytes=VMEM_LIMIT
        ),
        name="scatter",
    )(*saved)
    names = ("lift", "inner", "outer", "merge", "expand", "reduce")

    def finish(packed_ref, stem_ref, *rest):
        outs, stem_to = rest[:6], rest[6]
        stem_to[...] = stem_ref[...]
        for name, out in zip(names, outs):
            block, width = out.shape
            for slab in range(width // SLAB):
                start = plan[name] + slab * block
                out[:, slab * SLAB:(slab + 1) * SLAB] = packed_ref[start:start + block]

    outs = [jax.ShapeDtypeStruct(b, F32) for b in blocks] + [jax.ShapeDtypeStruct(full, F32)]
    return pl.pallas_call(
        finish,
        out_shape=tuple(outs),
        in_specs=[vmem, vmem],
        out_specs=tuple([vmem] * 7),
        compiler_params=pltpu.CompilerParams(vmem_limit_bytes=VMEM_LIMIT),
        name="finish",
    )(packed, stem)


def shards(stem_input, top_lower, top_upper, seed_lower, seed_upper, gamma_lower, gamma_upper, *weights):
    flat = lambda array: array.reshape(-1, array.shape[-1])
    weights = [w[0] for w in weights]
    saved = run_columns(
        flat(stem_input), flat(top_lower), flat(top_upper), flat(seed_lower), flat(seed_upper),
        gamma_lower, gamma_upper, weights,
    )
    factor = 1.0 / math.sqrt(saved[-1].shape[0] * lax.axis_size("dp"))
    results = run_scatter(saved, [w.shape for w in weights], factor)
    return tuple(r[None] for r in results[:6]) + (results[6].reshape(stem_input.shape),)


def solution(mesh):
    spread = P(None, "dp", None)
    gains = P("col", None)
    table = P("col", None, None)
    in_specs = (spread,) * 5 + (gains,) * 2 + (table,) * 6
    out_specs = (P("col", "dp", None),) * 6 + (spread,)
    return jax.shard_map(shards, mesh=mesh, in_specs=in_specs, out_specs=out_specs, check_vma=False)
```

```python
import functools
import math

import jax
import jax.numpy as jnp
from jax import lax
from jax.experimental import pallas as pl
from jax.experimental.pallas import tpu as pltpu
from jax.sharding import PartitionSpec as P

MESH = pl.DeviceIdType.MESH
F32 = jnp.float32
BF16 = jnp.bfloat16
EPS = 1e-06
PIECES = 16
FOLD = 4
VMEM_LIMIT = 60 << 20


def product(left, right):
    return jnp.dot(left, right, preferred_element_type=F32)


def right_outer(left, right):
    return lax.dot_general(left, right, (((1,), (1,)), ((), ())), preferred_element_type=F32)


def left_outer(left, right):
    return lax.dot_general(left, right, (((0,), (0,)), ((), ())), preferred_element_type=F32)


def inverse_rms(square_sum, width):
    return lax.rsqrt(square_sum * (1.0 / width) + EPS)


def row_sum(values):
    return jnp.sum(values, axis=-1, keepdims=True)


def norm_back(values, inverse, cotangent):
    normed = values * inverse
    mean = row_sum(cotangent * normed) * (1.0 / values.shape[-1])
    return inverse * (cotangent - normed * mean)


def gate(hidden):
    return 0.5 * jnp.tanh(0.5 * hidden) + 0.5


def column_kernel(
    pieces, columns,
    stem, top_lower, top_upper, seed_lower, seed_upper, gain_lower, gain_upper,
    lift, inner, outer, merge, expand, reduce,
    folded_out, merged_out, ugate_out, gu_out, duh_out, dmerged_out,
    ucast_out, dlift_out, normed_out, lgate_out, gl_out, dlh_out, part_half,
    in_low, in_up, in_glow, in_gup, out_low, out_up, out_glow, out_gup,
    slope_up, slope_low, top_half, send_sem, recv_sem, load_sem,
):
    column = lax.axis_index("col")
    first = column == columns - 1
    has_next = column > 0
    ru = in_up.shape[1]
    rl = FOLD * ru
    channels = in_low.shape[-1]
    lanes = channels // 2

    def half_copies(array, halves):
        return [
            pltpu.make_async_copy(
                array.at[:, pl.ds(h * lanes, lanes)], halves.at[h], load_sem.at[h]
            )
            for h in range(2)
        ]

    loads = half_copies(top_lower, top_half)

    @pl.when(first)
    def _():
        for load in loads:
            load.start()

    def strided(halves, start):
        return jnp.concatenate(
            [halves[h, pl.ds(start, ru, stride=FOLD), :] for h in range(2)], axis=1
        )

    streams = ((out_low, in_low), (out_up, in_up), (out_glow, in_glow), (out_gup, in_gup))

    def copy(kind, p):
        source, target = streams[kind]
        return pltpu.make_async_remote_copy(
            src_ref=source.at[p],
            dst_ref=target.at[p],
            send_sem=send_sem.at[kind, p],
            recv_sem=recv_sem.at[kind, p],
            device_id={"col": column - 1},
            device_id_type=MESH,
        )

    def push(kinds, p, role):
        if role != "last":
            for kind in kinds:
                copy(kind, p).start()

    def arrive(kind, p, role):
        if role != "first":
            copy(kind, p).wait_recv()

    inverse_gain_up = 1.0 / gain_upper[...]
    inverse_gain_low = 1.0 / gain_lower[...]

    @pl.when(first)
    def _():
        for load in loads:
            load.wait()

    spot = lax.broadcasted_iota(jnp.int32, (rl, rl), 0)
    token = lax.broadcasted_iota(jnp.int32, (rl, rl), 1)
    order = jnp.where(token == (spot % ru) * FOLD + spot // ru, 1.0, 0.0).astype(BF16)

    def piece(role, p, carry):
        base = p * rl

        if role == "first":
            seeds = product(order, seed_lower[p])
            for i in range(FOLD):
                in_low[p, i] = strided(top_half, base + i)
                in_glow[p, i] = seeds[i * ru:(i + 1) * ru]
            in_up[p] = top_upper[p]
            in_gup[p] = seed_upper[p].astype(F32)

        arrive(0, p, role)
        low = [in_low[p, i] for i in range(FOLD)]
        squares = sum(row_sum(v * v) for v in low)
        inverse_fold = inverse_rms(squares, FOLD * channels)
        folded = jnp.concatenate([(v * inverse_fold).astype(BF16) for v in low], axis=1)
        folded_out[p] = folded
        merged = product(folded, merge[...])
        inverse_merged = inverse_rms(row_sum(merged * merged), merged.shape[-1])
        merged_cast = (merged * inverse_merged).astype(BF16)
        merged_out[p] = merged_cast
        branch = jnp.zeros_like(merged)
        wide = expand.shape[1]
        step = wide
        for c in range(0, wide, step):
            hidden = product(merged_cast, expand[:, c:c + step])
            g = gate(hidden)
            gated = (hidden * g).astype(BF16)
            ugate_out[p, :, c:c + step] = gated
            slope_up[:, c:c + step] = g * (1.0 + hidden * (1.0 - g))
            branch = branch + product(gated, reduce[c:c + step, :])
        arrive(1, p, role)
        upper_prev = (in_up[p] - (merged + branch)) * inverse_gain_up
        out_up[p] = upper_prev
        upper_cast = upper_prev.astype(BF16)
        ucast_out[p] = upper_cast
        lifted = product(upper_cast, lift[...])
        mixed = product(order, stem[p]) + jnp.concatenate([lifted] * FOLD, axis=0)
        inverse_mixed = inverse_rms(row_sum(mixed * mixed), channels)
        normed = (mixed * inverse_mixed).astype(BF16)
        normed_out[p] = normed
        wide_low = inner.shape[1]
        lower_branch = jnp.zeros((rl, channels), F32)
        step_low = wide_low
        for c in range(0, wide_low, step_low):
            hidden = product(normed, inner[:, c:c + step_low])
            g = gate(hidden)
            gated = (hidden * g).astype(BF16)
            lgate_out[p, :, c:c + step_low] = gated
            slope_low[:, c:c + step_low] = g * (1.0 + hidden * (1.0 - g))
            lower_branch = lower_branch + product(gated, outer[c:c + step_low, :])
        for i in range(FOLD):
            out_low[p, i] = (in_low[p, i] - lower_branch[i * ru:(i + 1) * ru]) * inverse_gain_low
        push((0, 1), p, role)

        arrive(3, p, role)
        grad_up = in_gup[p]
        gu = grad_up.astype(BF16)
        gu_out[p] = gu
        d_cast = jnp.zeros_like(merged)
        for c in range(0, wide, step):
            d_gate = right_outer(gu, reduce[c:c + step, :])
            duh = (slope_up[:, c:c + step] * d_gate).astype(BF16)
            duh_out[p, :, c:c + step] = duh
            d_cast = d_cast + right_outer(duh, expand[:, c:c + step])
        dmerged = (grad_up + norm_back(merged, inverse_merged, d_cast)).astype(BF16)
        dmerged_out[p] = dmerged
        d_fold = right_outer(dmerged, merge[...])
        low = [in_low[p, i] * inverse_fold for i in range(FOLD)]
        parts = [d_fold[:, i * channels:(i + 1) * channels] for i in range(FOLD)]
        mean = sum(row_sum(a * b) for a, b in zip(low, parts)) * (1.0 / (FOLD * channels))
        arrive(2, p, role)
        total = []
        for i in range(FOLD):
            t = in_glow[p, i] + inverse_fold * (parts[i] - low[i] * mean)
            out_glow[p, i] = gain_lower[...] * t
            total.append(t.astype(BF16))
        gl = jnp.concatenate(total, axis=0)
        gl_out[p] = gl
        d_normed = jnp.zeros((rl, channels), F32)
        for c in range(0, wide_low, step_low):
            d_gate = right_outer(gl, outer[c:c + step_low, :])
            dlh = (slope_low[:, c:c + step_low] * d_gate).astype(BF16)
            dlh_out[p, :, c:c + step_low] = dlh
            d_normed = d_normed + right_outer(dlh, inner[:, c:c + step_low])
        d_mixed = norm_back(mixed, inverse_mixed, d_normed)
        d_lift = jnp.zeros((ru, channels), F32)
        for i in range(FOLD):
            part = d_mixed[i * ru:(i + 1) * ru]
            for h in range(2):
                part_half[h, pl.ds(base + i, ru, stride=FOLD), :] = part[:, h * lanes:(h + 1) * lanes]
            d_lift = d_lift + part
        d_lift = d_lift.astype(BF16)
        dlift_out[p] = d_lift
        out_gup[p] = gain_upper[...] * grad_up + right_outer(d_lift, lift[...])
        push((3, 2), p, role)
        return carry

    middle = jnp.logical_and(has_next, jnp.logical_not(first))
    roles = (("first", first), ("middle", middle), ("last", jnp.logical_not(has_next)))
    for role, here in roles:
        @pl.when(here)
        def _():
            lax.fori_loop(0, pieces, functools.partial(piece, role), 0)

    @pl.when(has_next)
    def _():
        def drain(p, carry):
            for kind in range(4):
                copy(kind, p).wait_send()
            return carry

        lax.fori_loop(0, pieces, drain, 0)


SLAB = 256


def scatter_kernel(
    columns, depth, factor, plan, rows_a,
    folded, merged, ugate, gu, duh, dmerged, ucast, dlift, normed, lgate, gl, dlh, stem_part,
    packed_out, stem_out,
    part, near, side, last, ring, stem_got, stem_half, stem_full,
    near_sem, side_sem, last_sem, ring_sem, row_sem, half_sem, full_sem, out_sem,
):
    column = lax.axis_index("col")
    place = lax.axis_index("dp")
    z, y, core = place // 4, (place // 2) % 2, place % 2
    at = lambda z, y, core: {"dp": z * 4 + y * 2 + core}
    peer = at(z, y, 1 - core)
    across = at(z, 1 - y, core)
    toward = (at((z + 1) % depth, y, core), at((z + depth - 1) % depth, y, core))
    row = columns // 2
    x, high = column % row, column // row
    mates = [(x + d) % row for d in range(1, row)]
    mate = lambda other: {"col": high * row + other}
    mirror = {"col": (1 - high) * row + x}

    def remote(source, target, send, recv, device):
        return pltpu.make_async_remote_copy(
            src_ref=source, dst_ref=target, send_sem=send, recv_sem=recv,
            device_id=device, device_id_type=MESH,
        )

    def weight_grad(name):
        left, right, start = {
            "reduce": (ugate, gu, plan["reduce"]), "expand": (merged, duh, plan["expand"]),
            "merge": (folded, dmerged, plan["merge"]), "outer": (lgate, gl, plan["outer"]),
            "inner": (normed, dlh, plan["inner"]), "lift": (ucast, dlift, plan["lift"]),
        }[name]
        height, width = left.shape[2], right.shape[2]
        whole = right[...].reshape(-1, width)
        block = height // (4 * depth)
        for top in range(0, height, SLAB):
            grad = left_outer(left[:, :, top:top + SLAB].reshape(-1, SLAB), whole)
            count = SLAB // (4 * block)
            z0 = top // (4 * block)
            for slab in range(width // SLAB):
                piece = grad[:, slab * SLAB:(slab + 1) * SLAB].reshape(count, 2, 2, block, SLAB)
                rows = slice(start + slab * block, start + (slab + 1) * block)
                for yb in range(2):
                    part[yb * depth + z0:yb * depth + z0 + count, :, rows, :] = piece[:, yb]

    a1, a2 = (0, plan["outer"], True, 0), (plan["outer"], rows_a - plan["outer"], True, 1)
    b1 = (rows_a, plan["merge"] - rows_a, False, 2)
    b2 = (plan["merge"], part.shape[2] - plan["merge"], False, 3)

    def near_copy(group):
        start, rows, _, number = group
        return remote(
            part.at[:, 1 - core, pl.ds(start, rows)], near.at[:, pl.ds(start, rows)],
            near_sem.at[0, number], near_sem.at[1, number], peer,
        )

    def side_copy(group):
        start, rows, _, number = group
        return remote(
            near.at[pl.ds((1 - y) * depth, depth), pl.ds(start, rows)],
            side.at[:, pl.ds(start - rows_a, rows)],
            side_sem.at[0, number - 2], side_sem.at[1, number - 2], across,
        )

    def flows(group):
        start, rows, first, number = group
        found = []
        for lane in range(2):
            for way in range(2):
                steps = depth // 2 if way == lane else depth // 2 - 1
                if first:
                    found.append((way, lane, steps, start, rows, lane, start, number))
                else:
                    half = rows // 2
                    slot = rows_a + (start - rows_a) // 2
                    found.append((way, lane, steps, start + lane * half, half, y, slot, number))
        return found

    def block_at(flow, step):
        way, steps = flow[0], flow[2]
        if way == 0:
            return (z + steps - step) % depth
        return (z + depth - steps + step) % depth

    def gathered(group, flow, zb):
        way, lane, steps, start, rows, yb, slot, number = flow
        value = near[yb * depth + zb, start:start + rows] + part[yb * depth + zb, core, start:start + rows]
        if not group[2]:
            value = value + side[zb, start - rows_a:start - rows_a + rows]
        return value

    def ring_copy(flow, step):
        way, lane, steps, start, rows, yb, slot, number = flow
        return remote(
            near.at[yb * depth + block_at(flow, step), pl.ds(start, rows)],
            ring.at[way, lane, step, pl.ds(slot, rows)],
            ring_sem.at[0, way, lane, step, number], ring_sem.at[1, way, lane, step, number],
            toward[way],
        )

    def ring_step(group, step):
        for flow in flows(group):
            way, lane, steps, start, rows, yb, slot, number = flow
            if step >= steps:
                continue
            zb = block_at(flow, step)
            value = gathered(group, flow, zb)
            if step > 0:
                ring_copy(flow, step - 1).wait_recv()
                value = value + ring[way, lane, step - 1, slot:slot + rows]
            near[yb * depth + zb, start:start + rows] = value
            ring_copy(flow, step).start()

    def ring_end(group):
        found = flows(group)
        for lane in range(2):
            pair = [flow for flow in found if flow[1] == lane]
            way, lane, steps, start, rows, yb, slot, number = pair[0]
            value = gathered(group, pair[0], z)
            for flow in pair:
                ring_copy(flow, flow[2] - 1).wait_recv()
                value = value + ring[flow[0], lane, flow[2] - 1, slot:slot + rows]
            near[yb * depth + z, start:start + rows] = value

    def side_open(group):
        start, rows, _, number = group

        def add(zb, carry):
            b = (1 - y) * depth + zb
            near[b, start:start + rows] = near[b, start:start + rows] + part[b, core, start:start + rows]
            return carry

        lax.fori_loop(0, depth, add, 0)
        side_copy(group).start()

    a1, a2 = (0, plan["outer"], True, 0), (plan["outer"], rows_a - plan["outer"], True, 1)
    b1 = (rows_a, plan["merge"] - rows_a, False, 2)
    b2 = (plan["merge"], part.shape[2] - plan["merge"], False, 3)

    quarter = stem_part.shape[1] // row
    half = quarter // 2
    span = lambda index, size: pl.ds(pl.multiple_of(index * size, size), size)

    def row_copy(target, slot):
        return remote(
            stem_part.at[:, span(target, quarter)], stem_got.at[slot],
            row_sem.at[0, target], row_sem.at[1, slot], mate(target),
        )

    half_copy = remote(
        stem_half.at[0, :, span(1 - high, half)], stem_half.at[1, :, pl.ds(0, half)],
        half_sem.at[0], half_sem.at[1], mirror,
    )

    def back_copy(part_of):
        ref = stem_full.at[x, :, span(part_of, half)]
        return remote(ref, ref, half_sem.at[2], half_sem.at[3], mirror)

    def full_copy(target, slot):
        ref = stem_full.at[slot]
        return remote(ref, ref, full_sem.at[0, target], full_sem.at[1, slot], mate(target))

    def stem_rows():
        total = stem_part[:, span(x, quarter), :]
        for other in mates:
            row_copy(other, other).wait_recv()
            total = total + stem_got[other]
        stem_half[0] = total
        half_copy.start()

    def stem_mirror():
        half_copy.wait_recv()
        stem_full[x, :, span(high, half), :] = (
            stem_half[0, :, span(high, half), :] + stem_half[1, :, 0:half]
        )
        back_copy(high).start()

    def stem_spread():
        back_copy(1 - high).wait_recv()
        for other in mates:
            full_copy(other, x).start()

    weight_grad("expand")
    near_copy(b1).start()
    weight_grad("reduce")
    near_copy(a1).start()
    near_copy(b1).wait_recv()
    side_open(b1)
    weight_grad("merge")
    near_copy(b2).start()
    near_copy(a1).wait_recv()
    ring_step(a1, 0)
    for name in ("outer", "inner", "lift"):
        weight_grad(name)
    near_copy(a2).start()
    near_copy(b2).wait_recv()
    side_open(b2)
    near_copy(a2).wait_recv()
    ring_step(a2, 0)
    for other in mates:
        row_copy(other, x).start()
    ring_step(a1, 1)
    ring_step(a2, 1)
    ring_step(a1, 2)
    ring_step(a2, 2)
    stem_rows()
    side_copy(b1).wait_recv()
    ring_step(b1, 0)
    ring_step(a1, 3)
    ring_step(a2, 3)
    stem_mirror()
    ring_step(b1, 1)
    ring_end(a1)
    ring_end(a2)
    last_copy = remote(
        near.at[(1 - y) * depth + z, pl.ds(0, rows_a)], last, last_sem.at[0], last_sem.at[1], across
    )
    last_copy.start()
    stem_spread()
    side_copy(b2).wait_recv()
    ring_step(b2, 0)
    for step in range(2, depth // 2):
        ring_step(b1, step)
        ring_step(b2, step - 1)
    ring_step(b2, depth // 2 - 1)
    for other in mates:
        full_copy(other, other).wait_recv()
    lanes = stem_full.shape[3]
    stem_stores = [
        pltpu.make_async_copy(
            stem_full.at[:, h], stem_out.at[:, :, pl.ds(h * lanes, lanes)], out_sem.at[h]
        )
        for h in range(2)
    ]
    for store in stem_stores:
        store.start()
    last_copy.wait_recv()
    packed_out[0:rows_a] = (near[y * depth + z, 0:rows_a] + last[...]) * factor
    ring_end(b1)
    ring_end(b2)
    packed_out[rows_a:] = near[y * depth + z, rows_a:] * factor

    for group in (a1, a2, b1, b2):
        near_copy(group).wait_send()
        for flow in flows(group):
            for step in range(flow[2]):
                ring_copy(flow, step).wait_send()
    for group in (b1, b2):
        side_copy(group).wait_send()
    last_copy.wait_send()
    half_copy.wait_send()
    back_copy(high).wait_send()
    for other in mates:
        row_copy(other, x).wait_send()
        full_copy(other, x).wait_send()
    for store in stem_stores:
        store.wait()


def whole_kernel(pieces, columns, depth, factor, plan, rows_a, *refs):
    inputs, outs, refs = refs[:13], refs[13:15], refs[15:]
    tables, load_sem, refs = refs[-7:-1], refs[-1], refs[:-7]
    loads = [
        pltpu.make_async_copy(source, table, load_sem.at[i])
        for i, (source, table) in enumerate(zip(inputs[7:], tables))
    ]
    for index in (3, 4, 5, 0, 1, 2):
        loads[index].start()
    saved, column_scratch, scatter_scratch = refs[:13], refs[13:27], refs[27:]
    column, place = lax.axis_index("col"), lax.axis_index("dp")
    z, y, core = place // 4, (place // 2) % 2, place % 2
    row = columns // 2
    x, high = column % row, column // row
    at = lambda z, y, core: {"dp": z * 4 + y * 2 + core}
    targets = [at(z, y, 1 - core), at(z, 1 - y, core)]
    targets += [at((z + 1) % depth, y, core), at((z + depth - 1) % depth, y, core)]
    targets += [{"col": (1 - high) * row + x}, {"col": columns - 1 - column}]
    targets += [{"col": high * row + (x + d) % row} for d in range(1, row)]
    barrier = pltpu.get_barrier_semaphore()
    for target in targets:
        pl.semaphore_signal(barrier, inc=1, device_id=target, device_id_type=MESH)

    pl.semaphore_wait(barrier, len(targets))
    for load in loads:
        load.wait()
    column_kernel(pieces, columns, *inputs[:7], *tables, *saved, *column_scratch)
    scatter_kernel(columns, depth, factor, plan, rows_a, *saved, *outs, *scatter_scratch)


def run(stem, top_lower, top_upper, seed_lower, seed_upper, gain_lower, gain_upper, weights, factor):
    pieces = PIECES
    lower_rows, channels = stem.shape
    upper_rows, width = top_upper.shape
    ru = upper_rows // pieces
    rl = lower_rows // pieces
    hidden_up = weights[4].shape[1]
    hidden_low = weights[1].shape[1]
    devices = lax.axis_size("dp")
    columns = lax.axis_size("col")
    depth = devices // 4
    blocks = [(w.shape[0] // devices, w.shape[1]) for w in weights]
    heights = {
        name: block * (cols // SLAB)
        for name, (block, cols) in zip(("lift", "inner", "outer", "merge", "expand", "reduce"), blocks)
    }
    plan, height = {}, 0
    for name in ("reduce", "outer", "inner", "lift", "expand", "merge"):
        plan[name] = height
        height += heights[name]
    rows_a = plan["expand"]
    slots = rows_a + (height - rows_a) // 2
    row = columns // 2
    quarter = lower_rows // row
    lanes = channels // 2
    full = (row, quarter, channels)
    kept = lambda rows, cols: pltpu.VMEM((pieces, rows, cols), BF16)
    low_slot = pltpu.VMEM((pieces, FOLD, ru, channels), F32)
    up_slot = pltpu.VMEM((pieces, ru, width), F32)
    half = pltpu.VMEM((2, lower_rows, lanes), F32)
    vmem = pl.BlockSpec(memory_space=pltpu.VMEM)
    away = pl.BlockSpec(memory_space=pl.ANY)
    dma = pltpu.SemaphoreType.DMA
    saved = [
        kept(ru, FOLD * channels), kept(ru, width), kept(ru, hidden_up), kept(ru, width),
        kept(ru, hidden_up), kept(ru, width), kept(ru, width), kept(ru, channels),
        kept(rl, channels), kept(rl, hidden_low), kept(rl, channels), kept(rl, hidden_low), half,
    ]
    column_scratch = [
        low_slot, up_slot, low_slot, up_slot, low_slot, up_slot, low_slot, up_slot,
        pltpu.VMEM((ru, hidden_up), F32), pltpu.VMEM((rl, hidden_low), F32), half,
        dma((4, pieces)), dma((4, pieces)), dma((2,)),
    ]
    scatter_scratch = [
        pltpu.VMEM((2 * depth, 2, height, SLAB), F32),
        pltpu.VMEM((2 * depth, height, SLAB), F32),
        pltpu.VMEM((depth, height - rows_a, SLAB), F32),
        pltpu.VMEM((rows_a, SLAB), F32),
        pltpu.VMEM((2, 2, depth // 2, slots, SLAB), F32),
        pltpu.VMEM((row, 2, quarter, lanes), F32), pltpu.VMEM((2, 2, quarter, lanes), F32),
        pltpu.VMEM((row, 2, quarter, lanes), F32),
        dma((2, 4)), dma((2, 2)), dma((2,)), dma((2, 2, 2, depth // 2, 4)),
        dma((2, row)), dma((4,)), dma((2, row)), dma((2,)),
    ]
    tables = [pltpu.VMEM(w.shape, BF16) for w in weights] + [dma((6,))]
    packed, stem_sum = pl.pallas_call(
        functools.partial(whole_kernel, pieces, columns, depth, factor, plan, rows_a),
        out_shape=(jax.ShapeDtypeStruct((height, SLAB), F32), jax.ShapeDtypeStruct(full, F32)),
        in_specs=[vmem, away] + [vmem] * 5 + [away] * 6,
        out_specs=(vmem, away),
        scratch_shapes=saved + column_scratch + scatter_scratch + tables,
        compiler_params=pltpu.CompilerParams(
            collective_id=0, has_side_effects=True, vmem_limit_bytes=VMEM_LIMIT
        ),
        name="columns",
    )(
        stem.reshape(pieces, rl, channels), top_lower, top_upper.reshape(pieces, ru, width),
        seed_lower.reshape(pieces, rl, channels), seed_upper.reshape(pieces, ru, width),
        gain_lower, gain_upper, *weights,
    )
    names = ("lift", "inner", "outer", "merge", "expand", "reduce")

    def finish(packed_ref, stem_ref, *rest):
        outs, stem_to = rest[:6], rest[6]
        stem_to[...] = stem_ref[...]
        for name, out in zip(names, outs):
            block, width = out.shape
            for slab in range(width // SLAB):
                start = plan[name] + slab * block
                out[:, slab * SLAB:(slab + 1) * SLAB] = packed_ref[start:start + block]

    outs = [jax.ShapeDtypeStruct(b, F32) for b in blocks] + [jax.ShapeDtypeStruct(full, F32)]
    return pl.pallas_call(
        finish,
        out_shape=tuple(outs),
        in_specs=[vmem, vmem],
        out_specs=tuple([vmem] * 7),
        compiler_params=pltpu.CompilerParams(vmem_limit_bytes=VMEM_LIMIT),
        name="finish",
    )(packed, stem_sum)


def shards(stem_input, top_lower, top_upper, seed_lower, seed_upper, gamma_lower, gamma_upper, *weights):
    flat = lambda array: array.reshape(-1, array.shape[-1])
    lower_rows = stem_input.shape[0] * stem_input.shape[1]
    results = run(
        flat(stem_input), flat(top_lower), flat(top_upper), flat(seed_lower), flat(seed_upper),
        gamma_lower, gamma_upper, [w[0] for w in weights],
        1.0 / math.sqrt(lower_rows * lax.axis_size("dp")),
    )
    return tuple(r[None] for r in results[:6]) + (results[6].reshape(stem_input.shape),)


def solution(mesh):
    spread = P(None, "dp", None)
    gains = P("col", None)
    table = P("col", None, None)
    in_specs = (spread,) * 5 + (gains,) * 2 + (table,) * 6
    out_specs = (P("col", "dp", None),) * 6 + (spread,)
    return jax.shard_map(shards, mesh=mesh, in_specs=in_specs, out_specs=out_specs, check_vma=False)
```

```python
import functools
import math

import jax
import jax.numpy as jnp
from jax import lax
from jax.experimental import pallas as pl
from jax.experimental.pallas import tpu as pltpu
from jax.sharding import PartitionSpec as P

MESH = pl.DeviceIdType.MESH
F32 = jnp.float32
BF16 = jnp.bfloat16
EPS = 1e-06
PIECES = 16
FOLD = 4
VMEM_LIMIT = 60 << 20


def product(left, right):
    return jnp.dot(left, right, preferred_element_type=F32)


def right_outer(left, right):
    return lax.dot_general(left, right, (((1,), (1,)), ((), ())), preferred_element_type=F32)


def left_outer(left, right):
    return lax.dot_general(left, right, (((0,), (0,)), ((), ())), preferred_element_type=F32)


def inverse_rms(square_sum, width):
    return lax.rsqrt(square_sum * (1.0 / width) + EPS)


def row_sum(values):
    return jnp.sum(values, axis=-1, keepdims=True)


def norm_back(values, inverse, cotangent):
    normed = values * inverse
    mean = row_sum(cotangent * normed) * (1.0 / values.shape[-1])
    return inverse * (cotangent - normed * mean)


def gate(hidden):
    return 0.5 * jnp.tanh(0.5 * hidden) + 0.5


def column_kernel(
    pieces, columns, table_loads,
    stem, top_lower, top_upper, seed_lower, seed_upper, gain_lower, gain_upper,
    lift, inner, outer, merge, expand, reduce,
    folded_out, merged_out, ugate_out, gu_out, duh_out, dmerged_out,
    ucast_out, dlift_out, normed_out, lgate_out, gl_out, dlh_out, part_half,
    in_low, in_up, in_glow, in_gup, out_low, out_up, out_glow, out_gup,
    slope_up, slope_low, top_half, send_sem, recv_sem, load_sem,
):
    column = lax.axis_index("col")
    first = column == columns - 1
    has_next = column > 0
    ru = in_up.shape[1]
    rl = FOLD * ru
    channels = in_low.shape[-1]
    lanes = channels // 2

    def half_copies(array, halves):
        return [
            pltpu.make_async_copy(
                array.at[:, pl.ds(h * lanes, lanes)], halves.at[h], load_sem.at[h]
            )
            for h in range(2)
        ]

    loads = half_copies(top_lower, top_half)

    @pl.when(first)
    def _():
        for load in loads:
            load.start()

    def strided(halves, start):
        return jnp.concatenate(
            [halves[h, pl.ds(start, ru, stride=FOLD), :] for h in range(2)], axis=1
        )

    streams = ((out_low, in_low), (out_up, in_up), (out_glow, in_glow), (out_gup, in_gup))

    def copy(kind, p):
        source, target = streams[kind]
        return pltpu.make_async_remote_copy(
            src_ref=source.at[p],
            dst_ref=target.at[p],
            send_sem=send_sem.at[kind],
            recv_sem=recv_sem.at[kind, p],
            device_id={"col": column - 1},
            device_id_type=MESH,
        )

    def push(kinds, p, role):
        if role != "last":
            for kind in kinds:
                copy(kind, p).start()

    def arrive(kind, p, role):
        if role != "first":
            copy(kind, p).wait_recv()

    inverse_gain_up = 1.0 / gain_upper[...]
    inverse_gain_low = 1.0 / gain_lower[...]

    @pl.when(first)
    def _():
        for load in loads:
            load.wait()

    for load in table_loads:
        load.wait()

    spot = lax.broadcasted_iota(jnp.int32, (rl, rl), 0)
    token = lax.broadcasted_iota(jnp.int32, (rl, rl), 1)
    order = jnp.where(token == (spot % ru) * FOLD + spot // ru, 1.0, 0.0).astype(BF16)

    def piece(role, p, carry):
        base = p * rl

        if role == "first":
            seeds = product(order, seed_lower[p])
            for i in range(FOLD):
                in_low[p, i] = strided(top_half, base + i)
                in_glow[p, i] = seeds[i * ru:(i + 1) * ru]
            in_up[p] = top_upper[p]
            in_gup[p] = seed_upper[p].astype(F32)

        arrive(0, p, role)
        low = [in_low[p, i] for i in range(FOLD)]
        squares = sum(row_sum(v * v) for v in low)
        inverse_fold = inverse_rms(squares, FOLD * channels)
        folded = jnp.concatenate([(v * inverse_fold).astype(BF16) for v in low], axis=1)
        folded_out[p] = folded
        merged = product(folded, merge[...])
        inverse_merged = inverse_rms(row_sum(merged * merged), merged.shape[-1])
        merged_cast = (merged * inverse_merged).astype(BF16)
        merged_out[p] = merged_cast
        branch = jnp.zeros_like(merged)
        wide = expand.shape[1]
        step = wide
        for c in range(0, wide, step):
            hidden = product(merged_cast, expand[:, c:c + step])
            g = gate(hidden)
            gated = (hidden * g).astype(BF16)
            ugate_out[p, :, c:c + step] = gated
            slope_up[:, c:c + step] = g * (1.0 + hidden * (1.0 - g))
            branch = branch + product(gated, reduce[c:c + step, :])
        arrive(1, p, role)
        upper_prev = (in_up[p] - (merged + branch)) * inverse_gain_up
        out_up[p] = upper_prev
        upper_cast = upper_prev.astype(BF16)
        ucast_out[p] = upper_cast
        lifted = product(upper_cast, lift[...])
        mixed = product(order, stem[p]) + jnp.concatenate([lifted] * FOLD, axis=0)
        inverse_mixed = inverse_rms(row_sum(mixed * mixed), channels)
        normed = (mixed * inverse_mixed).astype(BF16)
        normed_out[p] = normed
        wide_low = inner.shape[1]
        lower_branch = jnp.zeros((rl, channels), F32)
        step_low = wide_low
        for c in range(0, wide_low, step_low):
            hidden = product(normed, inner[:, c:c + step_low])
            g = gate(hidden)
            gated = (hidden * g).astype(BF16)
            lgate_out[p, :, c:c + step_low] = gated
            slope_low[:, c:c + step_low] = g * (1.0 + hidden * (1.0 - g))
            lower_branch = lower_branch + product(gated, outer[c:c + step_low, :])
        for i in range(FOLD):
            out_low[p, i] = (in_low[p, i] - lower_branch[i * ru:(i + 1) * ru]) * inverse_gain_low
        push((0, 1), p, role)

        arrive(3, p, role)
        grad_up = in_gup[p]
        gu = grad_up.astype(BF16)
        gu_out[p] = gu
        d_cast = jnp.zeros_like(merged)
        for c in range(0, wide, step):
            d_gate = right_outer(gu, reduce[c:c + step, :])
            duh = (slope_up[:, c:c + step] * d_gate).astype(BF16)
            duh_out[p, :, c:c + step] = duh
            d_cast = d_cast + right_outer(duh, expand[:, c:c + step])
        dmerged = (grad_up + norm_back(merged, inverse_merged, d_cast)).astype(BF16)
        dmerged_out[p] = dmerged
        d_fold = right_outer(dmerged, merge[...])
        low = [in_low[p, i] * inverse_fold for i in range(FOLD)]
        parts = [d_fold[:, i * channels:(i + 1) * channels] for i in range(FOLD)]
        mean = sum(row_sum(a * b) for a, b in zip(low, parts)) * (1.0 / (FOLD * channels))
        arrive(2, p, role)
        total = []
        for i in range(FOLD):
            t = in_glow[p, i] + inverse_fold * (parts[i] - low[i] * mean)
            out_glow[p, i] = gain_lower[...] * t
            total.append(t.astype(BF16))
        gl = jnp.concatenate(total, axis=0)
        gl_out[p] = gl
        d_normed = jnp.zeros((rl, channels), F32)
        for c in range(0, wide_low, step_low):
            d_gate = right_outer(gl, outer[c:c + step_low, :])
            dlh = (slope_low[:, c:c + step_low] * d_gate).astype(BF16)
            dlh_out[p, :, c:c + step_low] = dlh
            d_normed = d_normed + right_outer(dlh, inner[:, c:c + step_low])
        d_mixed = norm_back(mixed, inverse_mixed, d_normed)
        d_lift = jnp.zeros((ru, channels), F32)
        for i in range(FOLD):
            part = d_mixed[i * ru:(i + 1) * ru]
            for h in range(2):
                part_half[h, pl.ds(base + i, ru, stride=FOLD), :] = part[:, h * lanes:(h + 1) * lanes]
            d_lift = d_lift + part
        d_lift = d_lift.astype(BF16)
        dlift_out[p] = d_lift
        out_gup[p] = gain_upper[...] * grad_up + right_outer(d_lift, lift[...])
        push((3, 2), p, role)
        return carry

    middle = jnp.logical_and(has_next, jnp.logical_not(first))
    roles = (("first", first), ("middle", middle), ("last", jnp.logical_not(has_next)))
    for role, here in roles:
        @pl.when(here)
        def _():
            lax.fori_loop(0, pieces, functools.partial(piece, role), 0)

    @pl.when(has_next)
    def _():
        for kind, (source, target) in enumerate(streams):
            pltpu.make_async_remote_copy(
                src_ref=source, dst_ref=target, send_sem=send_sem.at[kind],
                recv_sem=recv_sem.at[kind, 0], device_id={"col": column - 1}, device_id_type=MESH,
            ).wait_send()


SLAB = 256


def scatter_kernel(
    columns, depth, factor, plan, rows_a,
    folded, merged, ugate, gu, duh, dmerged, ucast, dlift, normed, lgate, gl, dlh, stem_part,
    packed_out, stem_out,
    part, near, side, last, ring, stem_got, stem_half, stem_full,
    near_sem, side_sem, last_sem, ring_sem, row_sem, half_sem, full_sem, out_sem,
):
    column = lax.axis_index("col")
    place = lax.axis_index("dp")
    z, y, core = place // 4, (place // 2) % 2, place % 2
    at = lambda z, y, core: {"dp": z * 4 + y * 2 + core}
    peer = at(z, y, 1 - core)
    across = at(z, 1 - y, core)
    toward = (at((z + 1) % depth, y, core), at((z + depth - 1) % depth, y, core))
    row = columns // 2
    x, high = column % row, column // row
    mates = [(x + d) % row for d in range(1, row)]
    mate = lambda other: {"col": high * row + other}
    mirror = {"col": (1 - high) * row + x}

    def remote(source, target, send, recv, device):
        return pltpu.make_async_remote_copy(
            src_ref=source, dst_ref=target, send_sem=send, recv_sem=recv,
            device_id=device, device_id_type=MESH,
        )

    def weight_grad(name):
        left, right, start = {
            "reduce": (ugate, gu, plan["reduce"]), "expand": (merged, duh, plan["expand"]),
            "merge": (folded, dmerged, plan["merge"]), "outer": (lgate, gl, plan["outer"]),
            "inner": (normed, dlh, plan["inner"]), "lift": (ucast, dlift, plan["lift"]),
        }[name]
        height, width = left.shape[2], right.shape[2]
        whole = right[...].reshape(-1, width)
        block = height // (4 * depth)
        for top in range(0, height, SLAB):
            grad = left_outer(left[:, :, top:top + SLAB].reshape(-1, SLAB), whole)
            count = SLAB // (4 * block)
            z0 = top // (4 * block)
            for slab in range(width // SLAB):
                piece = grad[:, slab * SLAB:(slab + 1) * SLAB].reshape(count, 2, 2, block, SLAB)
                rows = slice(start + slab * block, start + (slab + 1) * block)
                for yb in range(2):
                    part[yb * depth + z0:yb * depth + z0 + count, :, rows, :] = piece[:, yb]

    a1, a2 = (0, plan["outer"], True, 0), (plan["outer"], rows_a - plan["outer"], True, 1)
    b1 = (rows_a, plan["merge"] - rows_a, False, 2)
    b2 = (plan["merge"], part.shape[2] - plan["merge"], False, 3)

    def near_copy(group):
        start, rows, _, number = group
        return remote(
            part.at[:, 1 - core, pl.ds(start, rows)], near.at[:, pl.ds(start, rows)],
            near_sem.at[0, number], near_sem.at[1, number], peer,
        )

    def side_copy(group):
        start, rows, _, number = group
        return remote(
            near.at[pl.ds((1 - y) * depth, depth), pl.ds(start, rows)],
            side.at[:, pl.ds(start - rows_a, rows)],
            side_sem.at[0, number - 2], side_sem.at[1, number - 2], across,
        )

    def flows(group):
        start, rows, first, number = group
        found = []
        for lane in range(2):
            for way in range(2):
                steps = depth // 2 if way == lane else depth // 2 - 1
                if first:
                    found.append((way, lane, steps, start, rows, lane, start, number))
                else:
                    half = rows // 2
                    slot = rows_a + (start - rows_a) // 2
                    found.append((way, lane, steps, start + lane * half, half, y, slot, number))
        return found

    def block_at(flow, step):
        way, steps = flow[0], flow[2]
        if way == 0:
            return (z + steps - step) % depth
        return (z + depth - steps + step) % depth

    def gathered(group, flow, zb):
        way, lane, steps, start, rows, yb, slot, number = flow
        value = near[yb * depth + zb, start:start + rows] + part[yb * depth + zb, core, start:start + rows]
        if not group[2]:
            value = value + side[zb, start - rows_a:start - rows_a + rows]
        return value

    def ring_copy(flow, step):
        way, lane, steps, start, rows, yb, slot, number = flow
        return remote(
            near.at[yb * depth + block_at(flow, step), pl.ds(start, rows)],
            ring.at[way, lane, step, pl.ds(slot, rows)],
            ring_sem.at[0, way, lane, step, number], ring_sem.at[1, way, lane, step, number],
            toward[way],
        )

    def ring_step(group, step):
        for flow in flows(group):
            way, lane, steps, start, rows, yb, slot, number = flow
            if step >= steps:
                continue
            zb = block_at(flow, step)
            value = gathered(group, flow, zb)
            if step > 0:
                ring_copy(flow, step - 1).wait_recv()
                value = value + ring[way, lane, step - 1, slot:slot + rows]
            near[yb * depth + zb, start:start + rows] = value
            ring_copy(flow, step).start()

    def ring_end(group):
        found = flows(group)
        for lane in range(2):
            pair = [flow for flow in found if flow[1] == lane]
            way, lane, steps, start, rows, yb, slot, number = pair[0]
            value = gathered(group, pair[0], z)
            for flow in pair:
                ring_copy(flow, flow[2] - 1).wait_recv()
                value = value + ring[flow[0], lane, flow[2] - 1, slot:slot + rows]
            near[yb * depth + z, start:start + rows] = value

    def side_open(group):
        start, rows, _, number = group

        def add(zb, carry):
            b = (1 - y) * depth + zb
            near[b, start:start + rows] = near[b, start:start + rows] + part[b, core, start:start + rows]
            return carry

        lax.fori_loop(0, depth, add, 0)
        side_copy(group).start()

    a1, a2 = (0, plan["outer"], True, 0), (plan["outer"], rows_a - plan["outer"], True, 1)
    b1 = (rows_a, plan["merge"] - rows_a, False, 2)
    b2 = (plan["merge"], part.shape[2] - plan["merge"], False, 3)

    quarter = stem_part.shape[1] // row
    half = quarter // 2
    span = lambda index, size: pl.ds(pl.multiple_of(index * size, size), size)

    def row_copy(target, slot):
        return remote(
            stem_part.at[:, span(target, quarter)], stem_got.at[slot],
            row_sem.at[0, target], row_sem.at[1, slot], mate(target),
        )

    half_copy = remote(
        stem_half.at[0, :, span(1 - high, half)], stem_half.at[1, :, pl.ds(0, half)],
        half_sem.at[0], half_sem.at[1], mirror,
    )

    def back_copy(part_of):
        ref = stem_full.at[x, :, span(part_of, half)]
        return remote(ref, ref, half_sem.at[2], half_sem.at[3], mirror)

    def full_copy(target, slot):
        ref = stem_full.at[slot]
        return remote(ref, ref, full_sem.at[0, target], full_sem.at[1, slot], mate(target))

    def stem_rows():
        total = stem_part[:, span(x, quarter), :]
        for other in mates:
            row_copy(other, other).wait_recv()
            total = total + stem_got[other]
        stem_half[0] = total
        half_copy.start()

    def stem_mirror():
        half_copy.wait_recv()
        stem_full[x, :, span(high, half), :] = (
            stem_half[0, :, span(high, half), :] + stem_half[1, :, 0:half]
        )
        back_copy(high).start()

    def stem_spread():
        back_copy(1 - high).wait_recv()
        for other in mates:
            full_copy(other, x).start()

    weight_grad("expand")
    near_copy(b1).start()
    weight_grad("reduce")
    near_copy(a1).start()
    near_copy(b1).wait_recv()
    side_open(b1)
    weight_grad("merge")
    near_copy(b2).start()
    near_copy(a1).wait_recv()
    ring_step(a1, 0)
    for name in ("outer", "inner", "lift"):
        weight_grad(name)
    near_copy(a2).start()
    near_copy(b2).wait_recv()
    side_open(b2)
    near_copy(a2).wait_recv()
    ring_step(a2, 0)
    for other in mates:
        row_copy(other, x).start()
    ring_step(a1, 1)
    ring_step(a2, 1)
    ring_step(a1, 2)
    ring_step(a2, 2)
    stem_rows()
    side_copy(b1).wait_recv()
    ring_step(b1, 0)
    ring_step(a1, 3)
    ring_step(a2, 3)
    stem_mirror()
    ring_step(b1, 1)
    ring_end(a1)
    ring_end(a2)
    last_copy = remote(
        near.at[(1 - y) * depth + z, pl.ds(0, rows_a)], last, last_sem.at[0], last_sem.at[1], across
    )
    last_copy.start()
    stem_spread()
    side_copy(b2).wait_recv()
    ring_step(b2, 0)
    for step in range(2, depth // 2):
        ring_step(b1, step)
        ring_step(b2, step - 1)
    ring_step(b2, depth // 2 - 1)
    for other in mates:
        full_copy(other, other).wait_recv()
    lanes = stem_full.shape[3]
    stem_stores = [
        pltpu.make_async_copy(
            stem_full.at[:, h], stem_out.at[:, :, pl.ds(h * lanes, lanes)], out_sem.at[h]
        )
        for h in range(2)
    ]
    for store in stem_stores:
        store.start()
    last_copy.wait_recv()
    packed_out[0:rows_a] = (near[y * depth + z, 0:rows_a] + last[...]) * factor
    ring_end(b1)
    ring_end(b2)
    packed_out[rows_a:] = near[y * depth + z, rows_a:] * factor

    for group in (a1, a2, b1, b2):
        near_copy(group).wait_send()
        for flow in flows(group):
            for step in range(flow[2]):
                ring_copy(flow, step).wait_send()
    for group in (b1, b2):
        side_copy(group).wait_send()
    last_copy.wait_send()
    half_copy.wait_send()
    back_copy(high).wait_send()
    for other in mates:
        row_copy(other, x).wait_send()
        full_copy(other, x).wait_send()
    for store in stem_stores:
        store.wait()


def whole_kernel(pieces, columns, depth, factor, plan, rows_a, *refs):
    inputs, outs, refs = refs[:13], refs[13:15], refs[15:]
    tables, load_sem, refs = refs[-7:-1], refs[-1], refs[:-7]
    loads = [
        pltpu.make_async_copy(source, table, load_sem.at[i])
        for i, (source, table) in enumerate(zip(inputs[7:], tables))
    ]
    for index in (3, 4, 5, 0, 1, 2):
        loads[index].start()
    saved, column_scratch, scatter_scratch = refs[:13], refs[13:27], refs[27:]
    column, place = lax.axis_index("col"), lax.axis_index("dp")
    z, y, core = place // 4, (place // 2) % 2, place % 2
    row = columns // 2
    x, high = column % row, column // row
    at = lambda z, y, core: {"dp": z * 4 + y * 2 + core}
    targets = [at(z, y, 1 - core), at(z, 1 - y, core)]
    targets += [at((z + 1) % depth, y, core), at((z + depth - 1) % depth, y, core)]
    targets += [{"col": (1 - high) * row + x}, {"col": columns - 1 - column}]
    targets += [{"col": high * row + (x + d) % row} for d in range(1, row)]
    barrier = pltpu.get_barrier_semaphore()
    for target in targets:
        pl.semaphore_signal(barrier, inc=1, device_id=target, device_id_type=MESH)

    pl.semaphore_wait(barrier, len(targets))
    column_kernel(pieces, columns, loads, *inputs[:7], *tables, *saved, *column_scratch)
    scatter_kernel(columns, depth, factor, plan, rows_a, *saved, *outs, *scatter_scratch)


def run(stem, top_lower, top_upper, seed_lower, seed_upper, gain_lower, gain_upper, weights, factor):
    pieces = PIECES
    lower_rows, channels = stem.shape
    upper_rows, width = top_upper.shape
    ru = upper_rows // pieces
    rl = lower_rows // pieces
    hidden_up = weights[4].shape[1]
    hidden_low = weights[1].shape[1]
    devices = lax.axis_size("dp")
    columns = lax.axis_size("col")
    depth = devices // 4
    blocks = [(w.shape[0] // devices, w.shape[1]) for w in weights]
    heights = {
        name: block * (cols // SLAB)
        for name, (block, cols) in zip(("lift", "inner", "outer", "merge", "expand", "reduce"), blocks)
    }
    plan, height = {}, 0
    for name in ("reduce", "outer", "inner", "lift", "expand", "merge"):
        plan[name] = height
        height += heights[name]
    rows_a = plan["expand"]
    slots = rows_a + (height - rows_a) // 2
    row = columns // 2
    quarter = lower_rows // row
    lanes = channels // 2
    full = (row, quarter, channels)
    kept = lambda rows, cols: pltpu.VMEM((pieces, rows, cols), BF16)
    low_slot = pltpu.VMEM((pieces, FOLD, ru, channels), F32)
    up_slot = pltpu.VMEM((pieces, ru, width), F32)
    half = pltpu.VMEM((2, lower_rows, lanes), F32)
    vmem = pl.BlockSpec(memory_space=pltpu.VMEM)
    away = pl.BlockSpec(memory_space=pl.ANY)
    dma = pltpu.SemaphoreType.DMA
    saved = [
        kept(ru, FOLD * channels), kept(ru, width), kept(ru, hidden_up), kept(ru, width),
        kept(ru, hidden_up), kept(ru, width), kept(ru, width), kept(ru, channels),
        kept(rl, channels), kept(rl, hidden_low), kept(rl, channels), kept(rl, hidden_low), half,
    ]
    column_scratch = [
        low_slot, up_slot, low_slot, up_slot, low_slot, up_slot, low_slot, up_slot,
        pltpu.VMEM((ru, hidden_up), F32), pltpu.VMEM((rl, hidden_low), F32), half,
        dma((4,)), dma((4, pieces)), dma((2,)),
    ]
    scatter_scratch = [
        pltpu.VMEM((2 * depth, 2, height, SLAB), F32),
        pltpu.VMEM((2 * depth, height, SLAB), F32),
        pltpu.VMEM((depth, height - rows_a, SLAB), F32),
        pltpu.VMEM((rows_a, SLAB), F32),
        pltpu.VMEM((2, 2, depth // 2, slots, SLAB), F32),
        pltpu.VMEM((row, 2, quarter, lanes), F32), pltpu.VMEM((2, 2, quarter, lanes), F32),
        pltpu.VMEM((row, 2, quarter, lanes), F32),
        dma((2, 4)), dma((2, 2)), dma((2,)), dma((2, 2, 2, depth // 2, 4)),
        dma((2, row)), dma((4,)), dma((2, row)), dma((2,)),
    ]
    tables = [pltpu.VMEM(w.shape, BF16) for w in weights] + [dma((6,))]
    packed, stem_sum = pl.pallas_call(
        functools.partial(whole_kernel, pieces, columns, depth, factor, plan, rows_a),
        out_shape=(jax.ShapeDtypeStruct((height, SLAB), F32), jax.ShapeDtypeStruct(full, F32)),
        in_specs=[vmem, away] + [vmem] * 5 + [away] * 6,
        out_specs=(vmem, away),
        scratch_shapes=saved + column_scratch + scatter_scratch + tables,
        compiler_params=pltpu.CompilerParams(
            collective_id=0, has_side_effects=True, vmem_limit_bytes=VMEM_LIMIT
        ),
        name="columns",
    )(
        stem.reshape(pieces, rl, channels), top_lower, top_upper.reshape(pieces, ru, width),
        seed_lower.reshape(pieces, rl, channels), seed_upper.reshape(pieces, ru, width),
        gain_lower, gain_upper, *weights,
    )
    names = ("lift", "inner", "outer", "merge", "expand", "reduce")

    def finish(packed_ref, stem_ref, *rest):
        outs, stem_to = rest[:6], rest[6]
        stem_to[...] = stem_ref[...]
        for name, out in zip(names, outs):
            block, width = out.shape
            for slab in range(width // SLAB):
                start = plan[name] + slab * block
                out[:, slab * SLAB:(slab + 1) * SLAB] = packed_ref[start:start + block]

    outs = [jax.ShapeDtypeStruct(b, F32) for b in blocks] + [jax.ShapeDtypeStruct(full, F32)]
    return pl.pallas_call(
        finish,
        out_shape=tuple(outs),
        in_specs=[vmem, vmem],
        out_specs=tuple([vmem] * 7),
        compiler_params=pltpu.CompilerParams(vmem_limit_bytes=VMEM_LIMIT),
        name="finish",
    )(packed, stem_sum)


def shards(stem_input, top_lower, top_upper, seed_lower, seed_upper, gamma_lower, gamma_upper, *weights):
    flat = lambda array: array.reshape(-1, array.shape[-1])
    lower_rows = stem_input.shape[0] * stem_input.shape[1]
    results = run(
        flat(stem_input), flat(top_lower), flat(top_upper), flat(seed_lower), flat(seed_upper),
        gamma_lower, gamma_upper, [w[0] for w in weights],
        1.0 / math.sqrt(lower_rows * lax.axis_size("dp")),
    )
    return tuple(r[None] for r in results[:6]) + (results[6].reshape(stem_input.shape),)


def solution(mesh):
    spread = P(None, "dp", None)
    gains = P("col", None)
    table = P("col", None, None)
    in_specs = (spread,) * 5 + (gains,) * 2 + (table,) * 6
    out_specs = (P("col", "dp", None),) * 6 + (spread,)
    return jax.shard_map(shards, mesh=mesh, in_specs=in_specs, out_specs=out_specs, check_vma=False)
```
